512 devices in a mesh: dp: 64 (over z, y), space: 8 (over x, core).
Axes of the slice: x: 4, y: 4, z: 16, core: 2. Of those that a mesh axis runs over, the one named last changes fastest.
Arguments:
- volume: bfloat16 [64, 4, 64, 8, 128], P('dp', None, 'space'), may hold values from -6 to 6
- w_first: bfloat16 [32, 4, 3, 3, 3], replicated, may hold values from -0.625 to 0.625
- b_first: float32 [32], replicated, may hold values from -0.5 to 0.5
- w_second: bfloat16 [64, 32, 3, 3, 3], replicated, may hold values from -0.21875 to 0.21875
- b_second: float32 [64], replicated, may hold values from -0.5 to 0.5
- cotangent: bfloat16 [64, 64, 16, 2, 32], P('dp', None, 'space'), may hold values from -1 to 1
Outputs:
- features: bfloat16 [64, 64, 16, 2, 32], P('dp', None, 'space')
- grad_w_first: float32 [32, 4, 3, 3, 3], replicated
- grad_b_first: float32 [32], replicated
- grad_w_second: float32 [64, 32, 3, 3, 3], replicated
- grad_b_second: float32 [64], replicated
The draws below stay inside these ranges and needn't reach their ends.
All inputs are finite; a program needn't handle non-finite values.
Results may differ from the reference program's by a relative error of at most 0.005.
The reference program's roundings to bfloat16 on the way (of `act_first`, `grad_second` and `grad_first`) count: a program that leaves them out, or rounds other values in their place, can miss the bound.
Values may be sent and summed in bfloat16 or wider, within the bound.
No kernel may reach another device: no remote copies, remote signals or barrier semaphores. Data moves between devices by JAX's collectives and lax.ppermute only.
A program may use at most 128 MiB of HBM per device.

```python
import math
import jax
import jax.numpy as jnp
from jax import lax

C_IN = 4
C_MID = 32
C_OUT = 64
Y = 8
X = 128
SAMPLES = 64
DEPTH = 64


def draw_cotangent(key, part):
    key = jax.random.fold_in(key, 11)
    shape = (SAMPLES, C_OUT, DEPTH // 4, Y // 4, X // 4)
    raw = jnp.clip(jax.random.normal(key, shape, jnp.float32), -3.0, 3.0)
    sample_pos = jnp.arange(SAMPLES, dtype=jnp.float32) / max(SAMPLES - 1, 1)
    depth_pos = jnp.arange(DEPTH // 4, dtype=jnp.float32) / max(DEPTH // 4 - 1, 1)
    rising = (3.0 ** sample_pos)[:, None, None, None, None] * (3.0 ** depth_pos)[None, None, :, None, None]
    factor = 24.0 / math.sqrt(SAMPLES * DEPTH * Y * X)
    return jnp.clip(raw * rising * factor, -1.0, 1.0).astype(jnp.bfloat16)


def steps_of(own_key, shape, shards, low, largest):
    def one(dim, parts):
        draws = jax.random.uniform(jax.random.fold_in(jax.random.fold_in(own_key, 6), dim), (parts,), jnp.float32, low / len(shards), largest / len(shards))
        return jnp.repeat(jnp.exp(draws), shape[dim] // parts).reshape((-1,) + (1,) * (len(shape) - dim - 1))

    loudness = one(*shards[0])
    for cut in shards[1:]:
        loudness = loudness * one(*cut)
    return loudness


def centred(stream_key, shape, spread, bound, split=(), held_as=jnp.bfloat16):
    loudness = steps_of(stream_key, shape, split, -0.22, 0.18) if split else 1.0
    drawn = jax.random.normal(stream_key, shape, jnp.float32) * spread * loudness
    return jnp.minimum(jnp.maximum(drawn, -bound), bound).astype(held_as)


def setup_inputs(seed: int = 0) -> dict:
    keys = jax.random.split(jax.random.key(seed), 7)
    return {
        "volume": centred(keys[0], (SAMPLES, C_IN, DEPTH, Y, X), 1.0, 6.0, ((0, 64), (2, 8))),
        "w_first": centred(keys[1], (C_MID, C_IN, 3, 3, 3), (27 * C_IN) ** -0.5, 0.625),
        "b_first": jnp.clip(jax.random.uniform(keys[2], (C_MID,), jnp.float32, -0.5, 0.5), -0.5, 0.5),
        "w_second": centred(keys[3], (C_OUT, C_MID, 3, 3, 3), (27 * C_MID) ** -0.5, 0.21875),
        "b_second": jnp.clip(jax.random.uniform(keys[4], (C_OUT,), jnp.float32, -0.5, 0.5), -0.5, 0.5),
        "cotangent": draw_cotangent(jax.random.fold_in(keys[6], 71), 0),
    }


def conv_valid(padded, weights):
    return lax.conv_general_dilated(padded[None], weights, (1, 1, 1), 'VALID', dimension_numbers=('NCDHW', 'OIDHW', 'NCDHW'), preferred_element_type=jnp.float32)[0]

def weight_grad(padded, upstream):
    result = lax.conv_general_dilated(padded[None], upstream[None], (1, 1, 1), 'VALID', dimension_numbers=('CNDHW', 'IODHW', 'NCDHW'), preferred_element_type=jnp.float32)
    return jnp.transpose(result, (1, 0, 2, 3, 4))

def flip_weights(weights):
    return jnp.flip(jnp.transpose(weights, (1, 0, 2, 3, 4)), axis=(2, 3, 4))

def pool_cells(values):
    shape = values.shape
    blocks = values.reshape(shape[0], shape[1] // 2, 2, shape[2] // 2, 2, shape[3] // 2, 2)
    return lax.optimization_barrier(jnp.mean(blocks, axis=(2, 4, 6)))

def squash(values):
    return pool_cells(jnp.where(values > 0.0, values, 0.3 * values))

def pad_all(values):
    return jnp.pad(values, ((0, 0), (1, 1), (1, 1), (1, 1)))

def reference(volume, w_first, b_first, w_second, b_second, cotangent):

    def one_sample(pair):
        sample, upstream = pair
        padded_in = pad_all(sample)
        pre_first = conv_valid(padded_in, w_first) + b_first[:, None, None, None]
        act_float, back_first = jax.vjp(squash, pre_first)
        act_first = act_float.astype(jnp.bfloat16)
        padded_act = pad_all(act_first)
        pre_second = conv_valid(padded_act, w_second) + b_second[:, None, None, None]
        pooled, back_second = jax.vjp(squash, pre_second)
        grad_second = back_second(upstream.astype(jnp.float32))[0].astype(jnp.bfloat16)
        grad_act = conv_valid(pad_all(grad_second), flip_weights(w_second))
        grad_first = back_first(grad_act)[0].astype(jnp.bfloat16)
        return (pooled.astype(jnp.bfloat16), weight_grad(padded_in, grad_first), lax.optimization_barrier(jnp.sum(grad_first, axis=(1, 2, 3), dtype=jnp.float32)), weight_grad(padded_act, grad_second), lax.optimization_barrier(jnp.sum(grad_second, axis=(1, 2, 3), dtype=jnp.float32)))
    results = lax.map(one_sample, (volume, cotangent))
    return (results[0], lax.optimization_barrier(jnp.sum(results[1], axis=0)), lax.optimization_barrier(jnp.sum(results[2], axis=0)), lax.optimization_barrier(jnp.sum(results[3], axis=0)), lax.optimization_barrier(jnp.sum(results[4], axis=0)))
```

```python
import jax
import jax.numpy as jnp
from jax import lax
from jax.experimental import pallas as pl
from jax.experimental.pallas import tpu as pltpu
from jax.sharding import Mesh, PartitionSpec as P

BF16, F32 = jnp.bfloat16, jnp.float32
VMEM = pl.BlockSpec(memory_space=pltpu.VMEM)
PARAMS = pltpu.CompilerParams(vmem_limit_bytes=48 * 1024 * 1024)
C_IN, C_MID, C_OUT, Y, X = 4, 32, 64, 8, 128
DEEP = 5
COT_AT = C_IN * DEEP
ONES_AT = COT_AT + 4
BLOCKS = ONES_AT + 1
ROWS_W2, ROWS_W1, ROWS_B2, ROWS_B1, ROWS = 0, 432, 472, 480, 512


def dot(a, b, dims=((1,), (0,))):
    return lax.dot_general(a, b, (dims, ((), ())), preferred_element_type=F32)


def iota(shape, dim):
    return lax.broadcasted_iota(jnp.int32, shape, dim)


def split(v):
    hi = v.astype(BF16)
    return hi, (v - hi.astype(F32)).astype(BF16)


def leaky(v):
    return jnp.where(v > 0.0, v, 0.3 * v)


def rolled(v, shift):
    return pltpu.roll(v, shift, 1)


def taps(v, period):
    place = iota(v.shape, 1) % period
    before = jnp.where(place == 0, 0.0, rolled(v, 1))
    after = jnp.where(place == period - 1, 0.0, rolled(v, v.shape[1] - 1))
    return before, v, after


def pack_kernel(vol, cot, up, down):
    for c in range(C_IN):
        up[c * DEEP : (c + 1) * DEEP] = vol[c, 8 - DEEP :]
        down[c * DEEP : (c + 1) * DEEP] = vol[c, :DEEP]
    for ref, d in ((up, 1), (down, 0)):
        both = jnp.concatenate([cot[d, 0].astype(F32), cot[d, 1].astype(F32)], axis=1)
        ref[COT_AT:ONES_AT] = both.reshape(4, 8, 128).astype(BF16)
        ref[ONES_AT] = jnp.ones((8, 128), BF16)


def bias_rows(bias, copies):
    hi = bias.astype(BF16).astype(F32)
    lo = (bias - hi).astype(BF16).astype(F32)
    rest = bias - hi - lo
    hi, lo, rest = (jnp.concatenate([v] * copies, axis=1) for v in (hi, lo, rest))
    row = iota((128, 256), 0)
    zero = jnp.zeros((128, 256), F32)
    return jnp.where(row == 0, hi, jnp.where(row == 1, lo, jnp.where(row == 2, rest, zero)))


def weights_kernel(w1, b1, w2, b2, t1, t2, t2g):
    wide = jnp.concatenate([w1[...]] * 4, axis=1)
    y_in = iota((8, 128), 0)
    lanes = iota((8, 128), 1) // C_MID
    blocks = []
    for kd in range(3):
        for kx in range(3):
            for c in range(C_IN):
                halves = []
                for half in range(2):
                    ky = y_in - (lanes + 4 * half) + 1
                    total = jnp.zeros((8, 128), F32)
                    for k in range(3):
                        at = ((kd * 3 + k) * 3 + kx) * C_IN + c
                        total = jnp.where(ky == k, wide[at : at + 1], total)
                    halves.append(total)
                blocks.append(jnp.concatenate(halves, axis=1))
    body = jnp.concatenate(blocks + [bias_rows(b1[...], 8)[:96]], axis=0)
    t1[...] = body.T.astype(BF16)
    nothing = jnp.zeros((C_MID, C_OUT), F32)
    for kd in range(3):
        for kx in range(3):
            w = [w2[(kd * 3 + ky) * 3 + kx].astype(F32) for ky in range(3)]
            pair = {
                a: jnp.concatenate([w[a] if a < 3 else nothing, w[a - 1] if a > 0 else nothing], axis=1)
                for a in range(4)
            }
            none = jnp.zeros((C_MID, 128), F32)
            block = jnp.concatenate(
                [
                    jnp.concatenate([pair.get(y - 2 * p + 1, none) for p in range(2)], axis=1)
                    for y in range(4)
                ],
                axis=0,
            )
            t2g[kd * 128 : (kd + 1) * 128, kx * 256 : (kx + 1) * 256] = block.astype(BF16)
            at = (kd * 3 + kx) * 128
            t2[:, at : at + 128] = block.T.astype(BF16)
    t2[:, 1152:] = bias_rows(b2[...], 4).T.astype(BF16)


def main_kernel(vol, before, behind, cot, t1, t2, t2g, feat, grads, p1, pre1, p2, g4x, g1):
    lane = iota((1, 128), 1)
    low = lane < 64

    for z in range(-5, 13):
        def plane(c):
            if z < 0:
                return before[c * DEEP + z + 5]
            if z >= 8:
                return behind[c * DEEP + z - 8]
            return vol[c, z]
        v = jnp.concatenate([plane(c).astype(F32) for c in range(C_IN)], axis=0)
        stack = jnp.concatenate(taps(v, 128), axis=0).astype(BF16)
        for kd in range(3):
            to = z - kd + 1 + 4
            if 0 <= to < 16:
                p1[kd * 96 : (kd + 1) * 96, to * 128 : (to + 1) * 128] = stack
    p1[288:, :] = jnp.ones((96, 2048), BF16)

    his, los = [], []
    for d in range(8):
        pre = dot(t1[...], p1[:, d * 256 : (d + 1) * 256])
        if 2 <= d < 6:
            pre1[:, (d - 2) * 256 : (d - 1) * 256] = pre
        act = leaky(pre).reshape(4, 2, C_MID, 256)
        act = (act[:, 0] + act[:, 1]).reshape(128, 256)
        hi, lo = split(act[:, :128] + act[:, 128:])
        his.append(hi)
        los.append(lo)

    row, col = iota((256, 128), 0), iota((256, 128), 1)
    pool = jnp.where((row // 128 == col // 64) & (row % 128 // 2 == col % 64), 0.125, 0.0).astype(BF16)
    m_before = before[ONES_AT].astype(F32)[:1]
    m_behind = behind[ONES_AT].astype(F32)[:1]
    for r in range(6):
        act = dot(jnp.concatenate([his[r], his[r + 2]], axis=1), pool)
        act = act + dot(jnp.concatenate([los[r], los[r + 2]], axis=1), pool)
        if r < 2:
            act = act * jnp.where(low, m_before, 1.0)
        if r >= 4:
            act = act * jnp.where(low, 1.0, m_behind)
        act = act.astype(BF16).astype(F32)
        stack = jnp.concatenate(taps(act, 64), axis=0).astype(BF16)
        for kd in range(3):
            to = r - kd
            if 0 <= to < 4:
                p2[kd * 384 : (kd + 1) * 384, to * 128 : (to + 1) * 128] = stack
    p2[1152:, :] = jnp.ones((128, 512), BF16)

    pre2 = dot(t2[...], p2[...])

    act = leaky(pre2[:, 128:384]).reshape(2, 2, C_OUT, 256)
    act = act[:, 0] + act[:, 1]
    act = act[:, :, :128] + act[:, :, 128:]
    row, col = iota((64, 128), 0), iota((64, 128), 1)
    pool = jnp.where((row // 32 == col // 64) & (row % 32 == col % 64 // 2), 0.125, 0.0).astype(BF16)
    for y in range(2):
        hi, lo = split(act[y])
        out = dot(pool, hi, ((1,), (1,))) + dot(pool, lo, ((1,), (1,)))
        for d in range(2):
            feat[d, y] = out[d * 32 : (d + 1) * 32].astype(BF16)

    pieces = [before[COT_AT:ONES_AT].astype(F32).reshape(32, 128)]
    for d in range(2):
        pieces.append(jnp.concatenate([cot[d, 0].astype(F32), cot[d, 1].astype(F32)], axis=1))
    pieces.append(behind[COT_AT:ONES_AT].astype(F32).reshape(32, 128))
    cots = jnp.concatenate(pieces, axis=0).T.astype(BF16)
    row, col = iota((128, 384), 0), iota((128, 384), 1)
    spread = jnp.where((row // 32 == col // 128 + col % 128 // 64) & (row % 32 == col % 64 // 2), 0.125, 0.0)
    up = dot(cots, spread.astype(BF16))
    up = jnp.concatenate([up[:, :256], up[:, 128:]], axis=1).reshape(2, 1, C_OUT, 512)
    mask = pre2.reshape(2, 2, C_OUT, 512) > 0.0
    grad = jnp.where(mask, up, 0.3 * up).reshape(256, 512).astype(BF16)
    for r in range(4):
        piece = grad[:, r * 128 : (r + 1) * 128].astype(F32)
        for kx, tap in enumerate(reversed(taps(piece, 64))):
            g4x[kx * 256 : (kx + 1) * 256, r * 128 : (r + 1) * 128] = tap.astype(BF16)

    back = dot(t2g[0:128], g4x[:, 256:512])
    back = back + dot(t2g[128:256], g4x[:, 128:384])
    back = back + dot(t2g[256:384], g4x[:, 0:256])
    one = back * 0.125
    less = 0.3 * one
    stack = jnp.concatenate([one[:, :128], one[:, 128:], less[:, :128], less[:, 128:]], axis=0)
    row, col = iota((128, 256), 0), iota((128, 256), 1)
    spread = jnp.where(row == col // 128 * 64 + col % 128 // 2, 1.0, 0.0).astype(BF16)
    wide = dot(stack.astype(BF16), spread)
    for z in range(8):
        a = z // 2
        at, half = (a % 2) * 128, (a // 2) * 128
        yes = wide[at : at + 128, half : half + 128].reshape(4, 1, C_MID, 128)
        no = wide[256 + at : 384 + at, half : half + 128].reshape(4, 1, C_MID, 128)
        mask = pre1[:, z * 128 : (z + 1) * 128].reshape(4, 2, C_MID, 128) > 0.0
        g1[:, z * 128 : (z + 1) * 128] = jnp.where(mask, yes, no).reshape(256, 128).astype(BF16)

    d2 = dot(p2[0:1168, 128:384], g4x[256:512, 128:384], ((1,), (1,)))
    for kd in range(3):
        for kx in range(3):
            base = (kd * 3 + kx) * 128
            def block(y, p):
                return d2[base + y * 32 : base + (y + 1) * 32, p * 128 : (p + 1) * 128]
            for ky in range(3):
                even = [block(y, p) for p in range(2) for y in [2 * p + ky - 1] if 0 <= y < 4]
                odd = [block(y, p) for p in range(2) for y in [2 * p + ky] if 0 <= y < 4]
                total = sum(even[1:], even[0]) + rolled(sum(odd[1:], odd[0]), 64)
                at = ROWS_W2 + ((kd * 3 + ky) * 3 + kx) * 16
                grads[at : at + 16] = jnp.where(low, total[:16], rolled(total[16:], 64))
    d = d2[1152:1160, :128] + d2[1152:1160, 128:]
    grads[ROWS_B2 : ROWS_B2 + 8] = d + rolled(d, 64)

    d1 = dot(p1[0:304, 512:1536], g1[...], ((1,), (1,)))
    body = d1[:288].reshape(36, 8, 256)
    ky = iota((1, 8, 256), 1) - iota((1, 8, 256), 2) // C_MID + 1
    total = jnp.zeros((36, 128), F32)
    for k in range(3):
        part = jnp.sum(jnp.where(ky == k, body, 0.0), axis=1)
        part = part[:, :128] + part[:, 128:]
        part = part + rolled(part, 64)
        part = part + rolled(part, 32)
        total = jnp.where(lane // 32 == k, part, total)
    grads[ROWS_W1 : ROWS_W1 + 40] = jnp.concatenate([total, jnp.zeros((4, 128), F32)], axis=0)
    d = d1[288:296, :128] + d1[288:296, 128:]
    d = d + rolled(d, 64)
    grads[ROWS_B1 : ROWS_B1 + 8] = d + rolled(d, 32)
    grads[ROWS_B1 + 8 :] = jnp.zeros((ROWS - ROWS_B1 - 8, 128), F32)


def unpack_kernel(grads, w1, b1, w2, b2):
    for t in range(27):
        block = grads[t * 16 : (t + 1) * 16]
        w2[t, 0:16] = block[:, :64]
        w2[t, 16:32] = rolled(block, 64)[:, :64]
    body = grads[ROWS_W1 : ROWS_W1 + 40]
    for ky in range(3):
        part = rolled(body, (128 - 32 * ky) % 128) if ky else body
        for kd in range(3):
            for kx in range(3):
                at = (kd * 3 + kx) * C_IN
                w1[(kd * 3 + ky) * 3 + kx] = part[at : at + C_IN, :C_MID]
    b2[...] = grads[ROWS_B2 : ROWS_B2 + 1, :C_OUT]
    b1[...] = grads[ROWS_B1 : ROWS_B1 + 1, :C_MID]


def call(kernel, outs, *args, scratch=()):
    return pl.pallas_call(
        kernel,
        out_shape=[jax.ShapeDtypeStruct(s, t) for s, t in outs],
        in_specs=[VMEM] * len(args),
        out_specs=[VMEM] * len(outs),
        scratch_shapes=[pltpu.VMEM(s, t) for s, t in scratch],
        compiler_params=PARAMS,
    )(*args)


def summed_over_devices(grads):
    near = ("y", "x", "core")
    count = lax.axis_size(near)
    pieces = lax.all_to_all(grads.reshape(count, ROWS // count, 128), near, 0, 0)
    mine = jnp.sum(pieces, axis=0)
    far = lax.axis_size("z")
    pieces = lax.all_to_all(jnp.broadcast_to(mine[None], (far,) + mine.shape), "z", 0, 0)
    mine = jnp.sum(pieces, axis=0)
    whole = lax.all_to_all(jnp.broadcast_to(mine[None], (count,) + mine.shape), near, 0, 0)
    return whole.reshape(ROWS, 128)


def local(volume, w_first, b_first, w_second, b_second, cotangent):
    vol = volume[0]
    cot = jnp.transpose(cotangent[0], (1, 2, 3, 0))
    w1 = jnp.transpose(w_first, (2, 3, 4, 1, 0)).reshape(27 * C_IN, C_MID).astype(F32)
    w2 = jnp.transpose(w_second, (2, 3, 4, 1, 0)).reshape(27, C_MID, C_OUT)
    up, down = call(pack_kernel, [((BLOCKS, 8, 128), BF16)] * 2, vol, cot)
    space = ("x", "core")
    count = lax.axis_size(space)
    before = lax.ppermute(up, space, [(i, i + 1) for i in range(count - 1)])
    behind = lax.ppermute(down, space, [(i + 1, i) for i in range(count - 1)])
    t1, t2, t2g = call(
        weights_kernel,
        [((256, 384), BF16), ((256, 1280), BF16), ((384, 768), BF16)],
        w1, b_first[None], w2, b_second[None],
    )
    feat, grads = call(
        main_kernel,
        [((2, 2, 32, C_OUT), BF16), ((ROWS, 128), F32)],
        vol, before, behind, cot, t1, t2, t2g,
        scratch=[
            ((384, 2048), BF16),
            ((256, 1024), F32),
            ((1280, 512), BF16),
            ((768, 512), BF16),
            ((256, 1024), BF16),
        ],
    )
    grads = summed_over_devices(grads)
    gw1, gb1, gw2, gb2 = call(
        unpack_kernel,
        [((27, C_IN, C_MID), F32), ((1, C_MID), F32), ((27, C_MID, C_OUT), F32), ((1, C_OUT), F32)],
        grads,
    )
    gw1 = jnp.transpose(gw1.reshape(3, 3, 3, C_IN, C_MID), (4, 3, 0, 1, 2))
    gw2 = jnp.transpose(gw2.reshape(3, 3, 3, C_MID, C_OUT), (4, 3, 0, 1, 2))
    return jnp.transpose(feat, (3, 0, 1, 2))[None], gw1, gb1[0], gw2, gb2[0]


def solution(mesh):
    dp, space = mesh.devices.shape
    y = 4 if dp % 4 == 0 else 1
    grid = Mesh(mesh.devices.reshape(dp // y, y, space // 2, 2), ("z", "y", "x", "core"))
    data = P(("z", "y"), None, ("x", "core"), None, None)
    return jax.shard_map(
        local,
        mesh=grid,
        in_specs=(data, P(), P(), P(), P(), data),
        out_specs=(data, P(), P(), P(), P()),
        check_vma=False,
    )
```

```python
import jax
import jax.numpy as jnp
from jax import lax
from jax.experimental import pallas as pl
from jax.experimental.pallas import tpu as pltpu
from jax.sharding import Mesh, PartitionSpec as P

BF16, F32 = jnp.bfloat16, jnp.float32
VMEM = pl.BlockSpec(memory_space=pltpu.VMEM)
PARAMS = pltpu.CompilerParams(vmem_limit_bytes=48 * 1024 * 1024)
C_IN, C_MID, C_OUT, Y, X = 4, 32, 64, 8, 128
DEEP = 5
COT_AT = C_IN * DEEP
ONES_AT = COT_AT + 4
BLOCKS = ONES_AT + 1
ROWS_W2, ROWS_W1, ROWS_B2, ROWS_B1, ROWS = 0, 432, 472, 480, 512


def dot(a, b, dims=((1,), (0,))):
    return lax.dot_general(a, b, (dims, ((), ())), preferred_element_type=F32)


def iota(shape, dim):
    return lax.broadcasted_iota(jnp.int32, shape, dim)


def leaky(v):
    return jnp.where(v > 0.0, v, 0.3 * v)


def rolled(v, shift):
    return pltpu.roll(v, shift, 1)


def paired(v):
    return ((v + rolled(v, v.shape[1] - 1)) * 0.125).astype(BF16)


def taps(v, period):
    place = iota(v.shape, 1) % period
    before = jnp.where(place == 0, 0.0, rolled(v, 1))
    after = jnp.where(place == period - 1, 0.0, rolled(v, v.shape[1] - 1))
    return before, v, after


def pack_kernel(vol_at, cot_at, w1_at, b1_at, w2_at, b2_at, across, inside, vol, cot, w1, b1, w2, b2, sems):
    pairs = ((vol_at, vol), (cot_at, cot), (w1_at, w1), (b1_at, b1), (w2_at, w2), (b2_at, b2))
    copies = [pltpu.make_async_copy(a, b, sems.at[i]) for i, (a, b) in enumerate(pairs)]
    for copy in copies:
        copy.start()
    across[ONES_AT] = jnp.ones((8, 128), BF16)
    inside[ONES_AT] = jnp.ones((8, 128), BF16)
    copies[0].wait()
    copies[1].wait()

    def fill(first, last):
        for c in range(C_IN):
            first[c * DEEP : (c + 1) * DEEP] = vol[c, :DEEP]
            last[c * DEEP : (c + 1) * DEEP] = vol[c, 8 - DEEP :]
        for ref, d in ((first, 0), (last, 1)):
            both = jnp.concatenate([cot[d, 0].astype(F32), cot[d, 1].astype(F32)], axis=1)
            ref[COT_AT:ONES_AT] = both.reshape(4, 8, 128).astype(BF16)

    core = lax.axis_index("core")
    pl.when(core == 0)(lambda: fill(across, inside))
    pl.when(core == 1)(lambda: fill(inside, across))
    for copy in copies[2:]:
        copy.wait()


def bias_rows(bias, copies):
    hi = bias.astype(BF16).astype(F32)
    lo = (bias - hi).astype(BF16).astype(F32)
    rest = bias - hi - lo
    hi, lo, rest = (jnp.concatenate([v] * copies, axis=1) for v in (hi, lo, rest))
    row = iota((128, 256), 0)
    zero = jnp.zeros((128, 256), F32)
    return jnp.where(row == 0, hi, jnp.where(row == 1, lo, jnp.where(row == 2, rest, zero)))


def weights_kernel(w1, b1, w2, b2, t1, t2, t2g):
    narrow = jnp.concatenate([w1[t].astype(F32) for t in range(27)], axis=0)
    wide = jnp.concatenate([narrow] * 4, axis=1)
    y_in = iota((8, 128), 0)
    lanes = iota((8, 128), 1) // C_MID
    blocks = []
    for kd in range(3):
        for kx in range(3):
            for c in range(C_IN):
                halves = []
                for half in range(2):
                    ky = y_in - (lanes + 4 * half) + 1
                    total = jnp.zeros((8, 128), F32)
                    for k in range(3):
                        at = ((kd * 3 + k) * 3 + kx) * C_IN + c
                        total = jnp.where(ky == k, wide[at : at + 1], total)
                    halves.append(total)
                blocks.append(jnp.concatenate(halves, axis=1))
    body = jnp.concatenate(blocks + [bias_rows(b1[...].reshape(1, C_MID), 8)[:96]], axis=0)
    t1[...] = body.T.astype(BF16)
    nothing = jnp.zeros((C_MID, C_OUT), F32)
    for kd in range(3):
        for kx in range(3):
            w = [w2[(kd * 3 + ky) * 3 + kx].astype(F32) for ky in range(3)]
            pair = {
                a: jnp.concatenate([w[a] if a < 3 else nothing, w[a - 1] if a > 0 else nothing], axis=1)
                for a in range(4)
            }
            none = jnp.zeros((C_MID, 128), F32)
            block = jnp.concatenate(
                [
                    jnp.concatenate([pair.get(y - 2 * p + 1, none) for p in range(2)], axis=1)
                    for y in range(4)
                ],
                axis=0,
            )
            t2g[kd * 128 : (kd + 1) * 128, kx * 256 : (kx + 1) * 256] = block.astype(BF16)
            at = (kd * 3 + kx) * 128
            t2[:, at : at + 128] = block.T.astype(BF16)
    t2[:, 1152:] = bias_rows(b2[...].reshape(1, C_OUT), 4).T.astype(BF16)


def main_kernel(vol, across, inside, cot, t1, t2, t2g, feat, grads, before, behind, p1, pre1, p2, g4x, g1):
    def place(first, second):
        before[...] = first[...]
        behind[...] = second[...]

    core = lax.axis_index("core")
    pl.when(core == 0)(lambda: place(across, inside))
    pl.when(core == 1)(lambda: place(inside, across))
    lane = iota((1, 128), 1)
    low = lane < 64

    for z in range(-5, 13):
        def plane(c):
            if z < 0:
                return before[c * DEEP + z + 5]
            if z >= 8:
                return behind[c * DEEP + z - 8]
            return vol[c, z]
        v = jnp.concatenate([plane(c).astype(F32) for c in range(C_IN)], axis=0)
        stack = jnp.concatenate(taps(v, 128), axis=0).astype(BF16)
        for kd in range(3):
            to = z - kd + 1 + 4
            if 0 <= to < 16:
                p1[kd * 96 : (kd + 1) * 96, to * 128 : (to + 1) * 128] = stack
    p1[288:, :] = jnp.ones((96, 2048), BF16)

    pooled = []
    for d in range(8):
        pre = dot(t1[...], p1[:, d * 256 : (d + 1) * 256])
        if 2 <= d < 6:
            pre1[:, (d - 2) * 256 : (d - 1) * 256] = pre
        act = leaky(pre).reshape(4, 2, C_MID, 256)
        act = (act[:, 0] + act[:, 1]).reshape(128, 256)
        pooled.append(paired(act[:, :128] + act[:, 128:]))

    row, col = iota((256, 128), 0), iota((256, 128), 1)
    pool = jnp.where((row // 128 == col // 64) & (row % 128 == col % 64 * 2), 1.0, 0.0).astype(BF16)
    m_before = before[ONES_AT].astype(F32)[:1]
    m_behind = behind[ONES_AT].astype(F32)[:1]
    for r in range(6):
        act = dot(jnp.concatenate([pooled[r], pooled[r + 2]], axis=1), pool)
        if r < 2:
            act = act * jnp.where(low, m_before, 1.0)
        if r >= 4:
            act = act * jnp.where(low, 1.0, m_behind)
        stack = jnp.concatenate(taps(act, 64), axis=0).astype(BF16)
        for kd in range(3):
            to = r - kd
            if 0 <= to < 4:
                p2[kd * 384 : (kd + 1) * 384, to * 128 : (to + 1) * 128] = stack
    p2[1152:, :] = jnp.ones((128, 512), BF16)

    pre2 = dot(t2[...], p2[...])

    act = leaky(pre2[:, 128:384]).reshape(2, 2, C_OUT, 256)
    act = act[:, 0] + act[:, 1]
    act = act[:, :, :128] + act[:, :, 128:]
    row, col = iota((64, 128), 0), iota((64, 128), 1)
    pool = jnp.where((row // 32 == col // 64) & (row % 32 * 2 == col % 64), 1.0, 0.0).astype(BF16)
    for y in range(2):
        out = dot(pool, paired(act[y]), ((1,), (1,)))
        for d in range(2):
            feat[d, y] = out[d * 32 : (d + 1) * 32].astype(BF16)

    pieces = [before[COT_AT:ONES_AT].astype(F32).reshape(32, 128)]
    for d in range(2):
        pieces.append(jnp.concatenate([cot[d, 0].astype(F32), cot[d, 1].astype(F32)], axis=1))
    pieces.append(behind[COT_AT:ONES_AT].astype(F32).reshape(32, 128))
    cots = jnp.concatenate(pieces, axis=0).T.astype(BF16)
    row, col = iota((128, 384), 0), iota((128, 384), 1)
    spread = jnp.where((row // 32 == col // 128 + col % 128 // 64) & (row % 32 == col % 64 // 2), 0.125, 0.0)
    up = dot(cots, spread.astype(BF16))
    up = jnp.concatenate([up[:, :256], up[:, 128:]], axis=1).reshape(2, 1, C_OUT, 512)
    mask = pre2.reshape(2, 2, C_OUT, 512) > 0.0
    grad = jnp.where(mask, up, 0.3 * up).reshape(256, 512).astype(BF16)
    for r in range(4):
        piece = grad[:, r * 128 : (r + 1) * 128].astype(F32)
        for kx, tap in enumerate(reversed(taps(piece, 64))):
            g4x[kx * 256 : (kx + 1) * 256, r * 128 : (r + 1) * 128] = tap.astype(BF16)

    back = dot(t2g[0:128], g4x[:, 256:512])
    back = back + dot(t2g[128:256], g4x[:, 128:384])
    back = back + dot(t2g[256:384], g4x[:, 0:256])
    one = back * 0.125
    less = 0.3 * one
    stack = jnp.concatenate([one[:, :128], one[:, 128:], less[:, :128], less[:, 128:]], axis=0)
    row, col = iota((128, 256), 0), iota((128, 256), 1)
    spread = jnp.where(row == col // 128 * 64 + col % 128 // 2, 1.0, 0.0).astype(BF16)
    wide = dot(stack.astype(BF16), spread)
    for z in range(8):
        a = z // 2
        at, half = (a % 2) * 128, (a // 2) * 128
        yes = wide[at : at + 128, half : half + 128].reshape(4, 1, C_MID, 128)
        no = wide[256 + at : 384 + at, half : half + 128].reshape(4, 1, C_MID, 128)
        mask = pre1[:, z * 128 : (z + 1) * 128].reshape(4, 2, C_MID, 128) > 0.0
        g1[:, z * 128 : (z + 1) * 128] = jnp.where(mask, yes, no).reshape(256, 128).astype(BF16)

    d2 = dot(p2[0:1168, 128:384], g4x[256:512, 128:384], ((1,), (1,)))
    for kd in range(3):
        for kx in range(3):
            base = (kd * 3 + kx) * 128
            def block(y, p):
                return d2[base + y * 32 : base + (y + 1) * 32, p * 128 : (p + 1) * 128]
            for ky in range(3):
                even = [block(y, p) for p in range(2) for y in [2 * p + ky - 1] if 0 <= y < 4]
                odd = [block(y, p) for p in range(2) for y in [2 * p + ky] if 0 <= y < 4]
                total = sum(even[1:], even[0]) + rolled(sum(odd[1:], odd[0]), 64)
                at = ROWS_W2 + ((kd * 3 + ky) * 3 + kx) * 16
                grads[at : at + 16] = jnp.where(low, total[:16], rolled(total[16:], 64))
    d = d2[1152:1160, :128] + d2[1152:1160, 128:]
    grads[ROWS_B2 : ROWS_B2 + 8] = d + rolled(d, 64)

    d1 = dot(p1[0:304, 512:1536], g1[...], ((1,), (1,)))
    body = d1[:288].reshape(36, 8, 256)
    ky = iota((1, 8, 256), 1) - iota((1, 8, 256), 2) // C_MID + 1
    total = jnp.zeros((36, 128), F32)
    for k in range(3):
        part = jnp.sum(jnp.where(ky == k, body, 0.0), axis=1)
        part = part[:, :128] + part[:, 128:]
        part = part + rolled(part, 64)
        part = part + rolled(part, 32)
        total = jnp.where(lane // 32 == k, part, total)
    grads[ROWS_W1 : ROWS_W1 + 40] = jnp.concatenate([total, jnp.zeros((4, 128), F32)], axis=0)
    d = d1[288:296, :128] + d1[288:296, 128:]
    d = d + rolled(d, 64)
    grads[ROWS_B1 : ROWS_B1 + 8] = d + rolled(d, 32)
    grads[ROWS_B1 + 8 :] = jnp.zeros((ROWS - ROWS_B1 - 8, 128), F32)


def unpack_kernel(grads, w1, b1, w2, b2):
    for t in range(27):
        block = grads[t * 16 : (t + 1) * 16]
        w2[t, 0:16] = block[:, :64]
        w2[t, 16:32] = rolled(block, 64)[:, :64]
    body = grads[ROWS_W1 : ROWS_W1 + 40]
    for ky in range(3):
        part = rolled(body, (128 - 32 * ky) % 128) if ky else body
        for kd in range(3):
            for kx in range(3):
                at = (kd * 3 + kx) * C_IN
                w1[(kd * 3 + ky) * 3 + kx] = part[at : at + C_IN, :C_MID]
    b2[...] = grads[ROWS_B2 : ROWS_B2 + 1, :C_OUT]
    b1[...] = grads[ROWS_B1 : ROWS_B1 + 1, :C_MID]


def call(kernel, outs, *args, scratch=(), place=pltpu.VMEM):
    return pl.pallas_call(
        kernel,
        out_shape=[jax.ShapeDtypeStruct(s, t) for s, t in outs],
        in_specs=[pl.BlockSpec(memory_space=place)] * len(args),
        out_specs=[VMEM] * len(outs),
        scratch_shapes=scratch,
        compiler_params=PARAMS,
    )(*args)


def summed_over_devices(grads):
    near = ("y", "x", "core")
    count = lax.axis_size(near)
    pieces = lax.all_to_all(grads.reshape(count, ROWS // count, 128), near, 0, 0)
    mine = jnp.sum(pieces, axis=0)
    far = lax.axis_size("z")
    pieces = lax.all_to_all(jnp.broadcast_to(mine[None], (far,) + mine.shape), "z", 0, 0)
    mine = jnp.sum(pieces, axis=0)
    whole = lax.all_to_all(jnp.broadcast_to(mine[None], (count,) + mine.shape), near, 0, 0)
    return whole.reshape(ROWS, 128)


def local(volume, w_first, b_first, w_second, b_second, cotangent):
    cot = jnp.transpose(cotangent[0], (1, 2, 3, 0))
    w1 = jnp.transpose(w_first, (2, 3, 4, 1, 0)).reshape(27, C_IN, C_MID)
    w2 = jnp.transpose(w_second, (2, 3, 4, 1, 0)).reshape(27, C_MID, C_OUT)
    args = [pltpu.with_memory_space_constraint(a, pltpu.HBM) for a in (volume[0], cot, w1, b_first, w2, b_second)]
    across, inside, vol, cot, w1, b1, w2, b2 = call(
        pack_kernel,
        [((BLOCKS, 8, 128), BF16)] * 2 + [(a.shape, a.dtype) for a in args],
        *args,
        scratch=[pltpu.SemaphoreType.DMA((len(args),))],
        place=pltpu.HBM,
    )
    space = ("x", "core")
    count = lax.axis_size(space)
    pairs = [(i, i + 1) for i in range(1, count - 1, 2)]
    across = lax.ppermute(across, space, pairs + [(j, i) for i, j in pairs])
    pairs = [(i, i + 1) for i in range(0, count, 2)]
    inside = lax.ppermute(inside, space, pairs + [(j, i) for i, j in pairs])
    t1, t2, t2g = call(
        weights_kernel,
        [((256, 384), BF16), ((256, 1280), BF16), ((384, 768), BF16)],
        w1, b1, w2, b2,
    )
    feat, grads = call(
        main_kernel,
        [((2, 2, 32, C_OUT), BF16), ((ROWS, 128), F32)],
        vol, across, inside, cot, t1, t2, t2g,
        scratch=[
            pltpu.VMEM((BLOCKS, 8, 128), BF16),
            pltpu.VMEM((BLOCKS, 8, 128), BF16),
            pltpu.VMEM((384, 2048), BF16),
            pltpu.VMEM((256, 1024), F32),
            pltpu.VMEM((1280, 512), BF16),
            pltpu.VMEM((768, 512), BF16),
            pltpu.VMEM((256, 1024), BF16),
        ],
    )
    grads = summed_over_devices(grads)
    gw1, gb1, gw2, gb2 = call(
        unpack_kernel,
        [((27, C_IN, C_MID), F32), ((1, C_MID), F32), ((27, C_MID, C_OUT), F32), ((1, C_OUT), F32)],
        grads,
    )
    gw1 = jnp.transpose(gw1.reshape(3, 3, 3, C_IN, C_MID), (4, 3, 0, 1, 2))
    gw2 = jnp.transpose(gw2.reshape(3, 3, 3, C_MID, C_OUT), (4, 3, 0, 1, 2))
    return jnp.transpose(feat, (3, 0, 1, 2))[None], gw1, gb1[0], gw2, gb2[0]


def solution(mesh):
    dp, space = mesh.devices.shape
    y = 4 if dp % 4 == 0 else 1
    grid = Mesh(mesh.devices.reshape(dp // y, y, space // 2, 2), ("z", "y", "x", "core"))
    data = P(("z", "y"), None, ("x", "core"), None, None)
    return jax.shard_map(
        local,
        mesh=grid,
        in_specs=(data, P(), P(), P(), P(), data),
        out_specs=(data, P(), P(), P(), P()),
        check_vma=False,
    )
```

```python
import jax
import jax.numpy as jnp
from jax import lax
from jax.experimental import pallas as pl
from jax.experimental.pallas import tpu as pltpu
from jax.sharding import Mesh, PartitionSpec as P

BF16, F32 = jnp.bfloat16, jnp.float32
VMEM = pl.BlockSpec(memory_space=pltpu.VMEM)
PARAMS = pltpu.CompilerParams(vmem_limit_bytes=48 * 1024 * 1024)
C_IN, C_MID, C_OUT, Y, X = 4, 32, 64, 8, 128
DEEP = 5
COT_AT = C_IN * DEEP
ONES_AT = COT_AT + 4
BLOCKS = ONES_AT + 1
ROWS_W2, ROWS_W1, ROWS_B, ROWS = 0, 432, 480, 512


def dot(a, b, dims=((1,), (0,))):
    return lax.dot_general(a, b, (dims, ((), ())), preferred_element_type=F32)


def iota(shape, dim):
    return lax.broadcasted_iota(jnp.int32, shape, dim)


def leaky(v):
    return jnp.maximum(v, 0.3 * v)


def rolled(v, shift):
    return pltpu.roll(v, shift, 1)


def paired(v):
    return ((v + rolled(v, v.shape[1] - 1)) * 0.125).astype(BF16)


def taps(v, period):
    place = iota(v.shape, 1) % period
    before = jnp.where(place == 0, 0.0, rolled(v, 1))
    after = jnp.where(place == period - 1, 0.0, rolled(v, v.shape[1] - 1))
    return before, v, after


def pack_kernel(vol_at, cot_at, w1_at, b1_at, w2_at, b2_at, across, inside, vol, cot, w1, b1, w2, b2, sems):
    pairs = ((vol_at, vol), (cot_at, cot), (w1_at, w1), (b1_at, b1), (w2_at, w2), (b2_at, b2))
    copies = [pltpu.make_async_copy(a, b, sems.at[i]) for i, (a, b) in enumerate(pairs)]
    for copy in copies:
        copy.start()
    across[ONES_AT] = jnp.ones((8, 128), BF16)
    inside[ONES_AT] = jnp.ones((8, 128), BF16)
    copies[0].wait()
    copies[1].wait()

    def fill(first, last):
        for c in range(C_IN):
            first[c * DEEP : (c + 1) * DEEP] = vol[c, :DEEP]
            last[c * DEEP : (c + 1) * DEEP] = vol[c, 8 - DEEP :]
        for ref, d in ((first, 0), (last, 1)):
            both = jnp.concatenate([cot[d, 0].astype(F32), cot[d, 1].astype(F32)], axis=1)
            ref[COT_AT:ONES_AT] = both.reshape(4, 8, 128).astype(BF16)

    core = lax.axis_index("core")
    pl.when(core == 0)(lambda: fill(across, inside))
    pl.when(core == 1)(lambda: fill(inside, across))
    for copy in copies[2:]:
        copy.wait()


def bias_rows(bias, copies):
    hi = bias.astype(BF16).astype(F32)
    lo = (bias - hi).astype(BF16).astype(F32)
    rest = bias - hi - lo
    hi, lo, rest = (jnp.concatenate([v] * copies, axis=1) for v in (hi, lo, rest))
    row = iota((128, 256), 0)
    zero = jnp.zeros((128, 256), F32)
    return jnp.where(row == 0, hi, jnp.where(row == 1, lo, jnp.where(row == 2, rest, zero)))


def weights_kernel(w1, b1, w2, b2, t1, t2, t2g):
    narrow = jnp.concatenate([w1[t].astype(F32) for t in range(27)], axis=0)
    wide = jnp.concatenate([narrow] * 4, axis=1)
    y_in = iota((8, 128), 0)
    lanes = iota((8, 128), 1) // C_MID
    blocks = []
    for kd in range(3):
        for kx in range(3):
            for c in range(C_IN):
                halves = []
                for half in range(2):
                    ky = y_in - (lanes + 4 * half) + 1
                    total = jnp.zeros((8, 128), F32)
                    for k in range(3):
                        at = ((kd * 3 + k) * 3 + kx) * C_IN + c
                        total = jnp.where(ky == k, wide[at : at + 1], total)
                    halves.append(total)
                blocks.append(jnp.concatenate(halves, axis=1))
    body = jnp.concatenate(blocks + [bias_rows(b1[...].reshape(1, C_MID), 8)[:96]], axis=0)
    t1[...] = body.T.astype(BF16)
    nothing = jnp.zeros((C_MID, C_OUT), F32)
    for kd in range(3):
        for kx in range(3):
            w = [w2[(kd * 3 + ky) * 3 + kx].astype(F32) for ky in range(3)]
            pair = {
                a: jnp.concatenate([w[a] if a < 3 else nothing, w[a - 1] if a > 0 else nothing], axis=1)
                for a in range(4)
            }
            none = jnp.zeros((C_MID, 128), F32)
            block = jnp.concatenate(
                [
                    jnp.concatenate([pair.get(y - 2 * p + 1, none) for p in range(2)], axis=1)
                    for y in range(4)
                ],
                axis=0,
            )
            t2g[kd * 128 : (kd + 1) * 128, kx * 256 : (kx + 1) * 256] = block.astype(BF16)
            at = (kd * 3 + kx) * 128
            t2[:, at : at + 128] = block.T.astype(BF16)
    t2[:, 1152:] = bias_rows(b2[...].reshape(1, C_OUT), 4).T.astype(BF16)


def main_kernel(vol, across, inside, cot, t1, t2, t2g, feat, grads, before, behind, p1, pre1, p2, g4x, g1):
    def place(first, second):
        before[...] = first[...]
        behind[...] = second[...]

    core = lax.axis_index("core")
    pl.when(core == 0)(lambda: place(across, inside))
    pl.when(core == 1)(lambda: place(inside, across))
    lane = iota((1, 128), 1)
    low = lane < 64

    for z in range(-5, 13):
        def plane(c):
            if z < 0:
                return before[c * DEEP + z + 5]
            if z >= 8:
                return behind[c * DEEP + z - 8]
            return vol[c, z]
        v = jnp.concatenate([plane(c).astype(F32) for c in range(C_IN)], axis=0)
        stack = jnp.concatenate(taps(v, 128), axis=0).astype(BF16)
        for kd in range(3):
            to = z - kd + 1 + 4
            if 0 <= to < 16:
                p1[kd * 96 : (kd + 1) * 96, to * 128 : (to + 1) * 128] = stack
    p1[288:, :] = jnp.ones((96, 2048), BF16)

    pooled = []
    for d in range(8):
        pre = dot(t1[...], p1[:, d * 256 : (d + 1) * 256])
        if 2 <= d < 6:
            pre1[:, (d - 2) * 256 : (d - 1) * 256] = pre
        act = leaky(pre).reshape(4, 2, C_MID, 256)
        act = (act[:, 0] + act[:, 1]).reshape(128, 256)
        pooled.append(paired(act[:, :128] + act[:, 128:]))

    row, col = iota((256, 128), 0), iota((256, 128), 1)
    pool = jnp.where((row // 128 == col // 64) & (row % 128 == col % 64 * 2), 1.0, 0.0).astype(BF16)
    m_before = before[ONES_AT].astype(F32)[:1]
    m_behind = behind[ONES_AT].astype(F32)[:1]
    for r in range(6):
        act = dot(jnp.concatenate([pooled[r], pooled[r + 2]], axis=1), pool)
        if r < 2:
            act = act * jnp.where(low, m_before, 1.0)
        if r >= 4:
            act = act * jnp.where(low, 1.0, m_behind)
        stack = jnp.concatenate(taps(act, 64), axis=0).astype(BF16)
        for kd in range(3):
            to = r - kd
            if 0 <= to < 4:
                p2[kd * 384 : (kd + 1) * 384, to * 128 : (to + 1) * 128] = stack
    p2[1152:, :] = jnp.ones((128, 512), BF16)

    pre2 = dot(t2[...], p2[...])

    act = leaky(pre2[:, 128:384]).reshape(2, 2, C_OUT, 256)
    act = act[:, 0] + act[:, 1]
    act = act[:, :, :128] + act[:, :, 128:]
    row, col = iota((64, 128), 0), iota((64, 128), 1)
    pool = jnp.where((row // 32 == col // 64) & (row % 32 * 2 == col % 64), 1.0, 0.0).astype(BF16)
    for y in range(2):
        out = dot(pool, paired(act[y]), ((1,), (1,)))
        for d in range(2):
            feat[d, y] = out[d * 32 : (d + 1) * 32].astype(BF16)

    pieces = [before[COT_AT:ONES_AT].astype(F32).reshape(32, 128)]
    for d in range(2):
        pieces.append(jnp.concatenate([cot[d, 0].astype(F32), cot[d, 1].astype(F32)], axis=1))
    pieces.append(behind[COT_AT:ONES_AT].astype(F32).reshape(32, 128))
    cots = jnp.concatenate(pieces, axis=0).T.astype(BF16)
    row, col = iota((128, 384), 0), iota((128, 384), 1)
    spread = jnp.where((row // 32 == col // 128 + col % 128 // 64) & (row % 32 == col % 64 // 2), 0.125, 0.0)
    up = dot(cots, spread.astype(BF16))
    up = jnp.concatenate([up[:, :256], up[:, 128:]], axis=1).reshape(2, 1, C_OUT, 512)
    mask = pre2.reshape(2, 2, C_OUT, 512) > 0.0
    grad = jnp.where(mask, up, 0.3 * up).reshape(256, 512).astype(BF16)
    for r in range(4):
        piece = grad[:, r * 128 : (r + 1) * 128].astype(F32)
        for kx, tap in enumerate(reversed(taps(piece, 64))):
            g4x[kx * 256 : (kx + 1) * 256, r * 128 : (r + 1) * 128] = tap.astype(BF16)

    back = dot(t2g[0:128], g4x[:, 256:512])
    back = back + dot(t2g[128:256], g4x[:, 128:384])
    back = back + dot(t2g[256:384], g4x[:, 0:256])
    one = back * 0.125
    less = 0.3 * one
    stack = jnp.concatenate([one[:, :128], one[:, 128:], less[:, :128], less[:, 128:]], axis=0)
    row, col = iota((128, 256), 0), iota((128, 256), 1)
    spread = jnp.where(row == col // 128 * 64 + col % 128 // 2, 1.0, 0.0).astype(BF16)
    wide = dot(stack.astype(BF16), spread)
    for z in range(8):
        a = z // 2
        at, half = (a % 2) * 128, (a // 2) * 128
        yes = wide[at : at + 128, half : half + 128].reshape(4, 1, C_MID, 128)
        no = wide[256 + at : 384 + at, half : half + 128].reshape(4, 1, C_MID, 128)
        mask = pre1[:, z * 128 : (z + 1) * 128].reshape(4, 2, C_MID, 128) > 0.0
        g1[:, z * 128 : (z + 1) * 128] = jnp.where(mask, yes, no).reshape(256, 128).astype(BF16)

    d2 = dot(p2[0:1168, 128:384], g4x[256:512, 128:384], ((1,), (1,)))
    for kd in range(3):
        for kx in range(3):
            base = (kd * 3 + kx) * 128
            def block(y, p):
                return d2[base + y * 32 : base + (y + 1) * 32, p * 128 : (p + 1) * 128]
            for ky in range(3):
                even = [block(y, p) for p in range(2) for y in [2 * p + ky - 1] if 0 <= y < 4]
                odd = [block(y, p) for p in range(2) for y in [2 * p + ky] if 0 <= y < 4]
                total = sum(even[1:], even[0]) + rolled(sum(odd[1:], odd[0]), 64)
                at = ROWS_W2 + ((kd * 3 + ky) * 3 + kx) * 16
                grads[at : at + 16] = jnp.where(low, total[:16], rolled(total[16:], 64)).astype(BF16)
    bias2 = d2[1152:1160, :128] + d2[1152:1160, 128:]
    bias2 = bias2 + rolled(bias2, 64)

    d1 = dot(p1[0:304, 512:1536], g1[...], ((1,), (1,)))
    body = d1[:288].reshape(36, 8, 256)
    ky = iota((1, 8, 256), 1) - iota((1, 8, 256), 2) // C_MID + 1
    total = jnp.zeros((36, 128), F32)
    for k in range(3):
        part = jnp.sum(jnp.where(ky == k, body, 0.0), axis=1)
        part = part[:, :128] + part[:, 128:]
        part = part + rolled(part, 64)
        part = part + rolled(part, 32)
        total = jnp.where(lane // 32 == k, part, total)
    total = jnp.concatenate([total, jnp.zeros((12, 128), F32)], axis=0)
    grads[ROWS_W1 : ROWS_W1 + 48] = total.astype(BF16)
    bias1 = d1[288:296, :128] + d1[288:296, 128:]
    bias1 = bias1 + rolled(bias1, 64)
    bias1 = bias1 + rolled(bias1, 32)
    grads[ROWS_B : ROWS_B + 16] = jnp.concatenate([bias2, bias1], axis=0).astype(BF16)
    grads[ROWS_B + 16 :] = jnp.zeros((ROWS - ROWS_B - 16, 128), BF16)


def unpack_kernel(grads, w1, b1, w2, b2):
    for t in range(27):
        block = grads[t * 16 : (t + 1) * 16].astype(F32)
        w2[t, 0:16] = block[:, :64]
        w2[t, 16:32] = rolled(block, 64)[:, :64]
    body = grads[ROWS_W1 : ROWS_W1 + 48].astype(F32)
    for ky in range(3):
        part = rolled(body, (128 - 32 * ky) % 128) if ky else body
        for kd in range(3):
            for kx in range(3):
                at = (kd * 3 + kx) * C_IN
                w1[(kd * 3 + ky) * 3 + kx] = part[at : at + C_IN, :C_MID]
    body = grads[ROWS_B : ROWS_B + 16].astype(F32)
    b2[...] = body[:1, :C_OUT]
    b1[...] = body[8:9, :C_MID]


def call(kernel, outs, *args, scratch=(), place=pltpu.VMEM):
    return pl.pallas_call(
        kernel,
        out_shape=[jax.ShapeDtypeStruct(s, t) for s, t in outs],
        in_specs=[pl.BlockSpec(memory_space=place)] * len(args),
        out_specs=[VMEM] * len(outs),
        scratch_shapes=scratch,
        compiler_params=PARAMS,
    )(*args)


def sum_kernel(pieces, out):
    total = pieces[0].astype(F32)
    for i in range(1, pieces.shape[0]):
        total = total + pieces[i].astype(F32)
    total = total.astype(BF16)
    for i in range(out.shape[0]):
        out[i] = total


def summed_over_devices(grads):
    near = ("y", "x", "core")
    count, far = lax.axis_size(near), lax.axis_size("z")
    rows = ROWS // count
    pieces = lax.all_to_all(grads.reshape(count, rows, 128), near, 0, 0)
    (mine,) = call(sum_kernel, [((far, rows, 128), BF16)], pieces)
    pieces = lax.all_to_all(mine, "z", 0, 0)
    (mine,) = call(sum_kernel, [((count, rows, 128), BF16)], pieces)
    return lax.all_to_all(mine, near, 0, 0).reshape(ROWS, 128)


def local(volume, w_first, b_first, w_second, b_second, cotangent):
    cot = jnp.transpose(cotangent[0], (1, 2, 3, 0))
    w1 = jnp.transpose(w_first, (2, 3, 4, 1, 0)).reshape(27, C_IN, C_MID)
    w2 = jnp.transpose(w_second, (2, 3, 4, 1, 0)).reshape(27, C_MID, C_OUT)
    args = [pltpu.with_memory_space_constraint(a, pltpu.HBM) for a in (volume[0], cot, w1, b_first, w2, b_second)]
    across, inside, vol, cot, w1, b1, w2, b2 = call(
        pack_kernel,
        [((BLOCKS, 8, 128), BF16)] * 2 + [(a.shape, a.dtype) for a in args],
        *args,
        scratch=[pltpu.SemaphoreType.DMA((len(args),))],
        place=pltpu.HBM,
    )
    space = ("x", "core")
    count = lax.axis_size(space)
    pairs = [(i, i + 1) for i in range(1, count - 1, 2)]
    across = lax.ppermute(across, space, pairs + [(j, i) for i, j in pairs])
    pairs = [(i, i + 1) for i in range(0, count, 2)]
    inside = lax.ppermute(inside, space, pairs + [(j, i) for i, j in pairs])
    t1, t2, t2g = call(
        weights_kernel,
        [((256, 384), BF16), ((256, 1280), BF16), ((384, 768), BF16)],
        w1, b1, w2, b2,
    )
    feat, grads = call(
        main_kernel,
        [((2, 2, 32, C_OUT), BF16), ((ROWS, 128), BF16)],
        vol, across, inside, cot, t1, t2, t2g,
        scratch=[
            pltpu.VMEM((BLOCKS, 8, 128), BF16),
            pltpu.VMEM((BLOCKS, 8, 128), BF16),
            pltpu.VMEM((384, 2048), BF16),
            pltpu.VMEM((256, 1024), F32),
            pltpu.VMEM((1280, 512), BF16),
            pltpu.VMEM((768, 512), BF16),
            pltpu.VMEM((256, 1024), BF16),
        ],
    )
    grads = summed_over_devices(grads)
    gw1, gb1, gw2, gb2 = call(
        unpack_kernel,
        [((27, C_IN, C_MID), F32), ((1, C_MID), F32), ((27, C_MID, C_OUT), F32), ((1, C_OUT), F32)],
        grads,
    )
    gw1 = jnp.transpose(gw1.reshape(3, 3, 3, C_IN, C_MID), (4, 3, 0, 1, 2))
    gw2 = jnp.transpose(gw2.reshape(3, 3, 3, C_MID, C_OUT), (4, 3, 0, 1, 2))
    return jnp.transpose(feat, (3, 0, 1, 2))[None], gw1, gb1[0], gw2, gb2[0]


def solution(mesh):
    dp, space = mesh.devices.shape
    y = 4 if dp % 4 == 0 else 1
    grid = Mesh(mesh.devices.reshape(dp // y, y, space // 2, 2), ("z", "y", "x", "core"))
    data = P(("z", "y"), None, ("x", "core"), None, None)
    return jax.shard_map(
        local,
        mesh=grid,
        in_specs=(data, P(), P(), P(), P(), data),
        out_specs=(data, P(), P(), P(), P()),
        check_vma=False,
    )
```

```python
import jax
import jax.numpy as jnp
from jax import lax
from jax.experimental import pallas as pl
from jax.experimental.pallas import tpu as pltpu
from jax.sharding import Mesh, PartitionSpec as P

BF16, F32 = jnp.bfloat16, jnp.float32
VMEM = pl.BlockSpec(memory_space=pltpu.VMEM)
PARAMS = pltpu.CompilerParams(vmem_limit_bytes=48 * 1024 * 1024)
C_IN, C_MID, C_OUT, Y, X = 4, 32, 64, 8, 128
DEEP = 5
COT_AT = C_IN * DEEP
ONES_AT = COT_AT + 4
BLOCKS = ONES_AT + 1
ROWS_W2, ROWS_W1, ROWS_B2, ROWS_B1, ROWS = 0, 432, 480, 496, 512


def dot(a, b, dims=((1,), (0,))):
    return lax.dot_general(a, b, (dims, ((), ())), preferred_element_type=F32)


def iota(shape, dim):
    return lax.broadcasted_iota(jnp.int32, shape, dim)


def leaky(v):
    return jnp.maximum(v, 0.3 * v)


def rolled(v, shift):
    return pltpu.roll(v, shift, 1)


def paired(v):
    return ((v + rolled(v, v.shape[1] - 1)) * 0.125).astype(BF16)


def bias_scale():
    return 1.0 + iota((16, 128), 0).astype(F32) * 0.0625


def taps(v, period):
    place = iota(v.shape, 1) % period
    before = jnp.where(place == 0, 0.0, rolled(v, 1))
    after = jnp.where(place == period - 1, 0.0, rolled(v, v.shape[1] - 1))
    return before, v, after


def pack_kernel(vol_at, cot_at, w1_at, b1_at, w2_at, b2_at, inside, across, vol, cot, w1, b1, w2, b2, sems):
    pairs = ((vol_at, vol), (cot_at, cot), (w1_at, w1), (b1_at, b1), (w2_at, w2), (b2_at, b2))
    copies = [pltpu.make_async_copy(a, b, sems.at[i]) for i, (a, b) in enumerate(pairs)]
    for copy in copies:
        copy.start()
    across[ONES_AT] = jnp.ones((8, 128), BF16)
    inside[ONES_AT] = jnp.ones((8, 128), BF16)
    copies[0].wait()
    copies[1].wait()

    def fill(first, last):
        for c in range(C_IN):
            first[c * DEEP : (c + 1) * DEEP] = vol[c, :DEEP]
            last[c * DEEP : (c + 1) * DEEP] = vol[c, 8 - DEEP :]
        for ref, d in ((first, 0), (last, 1)):
            both = jnp.concatenate([cot[d, 0].astype(F32), cot[d, 1].astype(F32)], axis=1)
            ref[COT_AT:ONES_AT] = both.reshape(4, 8, 128).astype(BF16)

    core = lax.axis_index("core")
    pl.when(core == 0)(lambda: fill(across, inside))
    pl.when(core == 1)(lambda: fill(inside, across))
    for copy in copies[2:]:
        copy.wait()


def bias_rows(bias, copies):
    hi = bias.astype(BF16).astype(F32)
    lo = (bias - hi).astype(BF16).astype(F32)
    rest = bias - hi - lo
    hi, lo, rest = (jnp.concatenate([v] * copies, axis=1) for v in (hi, lo, rest))
    row = iota((128, 256), 0)
    zero = jnp.zeros((128, 256), F32)
    return jnp.where(row == 0, hi, jnp.where(row == 1, lo, jnp.where(row == 2, rest, zero)))


def weights_kernel(w1, b1, w2, b2, t1, t2, t2g):
    narrow = jnp.concatenate([w1[t].astype(F32) for t in range(27)], axis=0)
    wide = jnp.concatenate([narrow] * 4, axis=1)
    y_in = iota((8, 128), 0)
    lanes = iota((8, 128), 1) // C_MID
    blocks = []
    for kd in range(3):
        for kx in range(3):
            for c in range(C_IN):
                halves = []
                for half in range(2):
                    ky = y_in - (lanes + 4 * half) + 1
                    total = jnp.zeros((8, 128), F32)
                    for k in range(3):
                        at = ((kd * 3 + k) * 3 + kx) * C_IN + c
                        total = jnp.where(ky == k, wide[at : at + 1], total)
                    halves.append(total)
                blocks.append(jnp.concatenate(halves, axis=1))
    body = jnp.concatenate(blocks + [bias_rows(b1[...].reshape(1, C_MID), 8)[:96]], axis=0)
    t1[...] = body.T.astype(BF16)
    nothing = jnp.zeros((C_MID, C_OUT), F32)
    for kd in range(3):
        for kx in range(3):
            w = [w2[(kd * 3 + ky) * 3 + kx].astype(F32) for ky in range(3)]
            pair = {
                a: jnp.concatenate([w[a] if a < 3 else nothing, w[a - 1] if a > 0 else nothing], axis=1)
                for a in range(4)
            }
            none = jnp.zeros((C_MID, 128), F32)
            block = jnp.concatenate(
                [
                    jnp.concatenate([pair.get(y - 2 * p + 1, none) for p in range(2)], axis=1)
                    for y in range(4)
                ],
                axis=0,
            )
            t2g[kd * 128 : (kd + 1) * 128, kx * 256 : (kx + 1) * 256] = block.astype(BF16)
            at = (kd * 3 + kx) * 128
            t2[:, at : at + 128] = block.T.astype(BF16)
    t2[:, 1152:] = bias_rows(b2[...].reshape(1, C_OUT), 4).T.astype(BF16)


def main_kernel(vol, inside, across, cot, t1, t2, t2g, feat, grads, before, behind, p1, pre1, p2, g4x, g1):
    def place(first, second):
        before[...] = first[...]
        behind[...] = second[...]

    core = lax.axis_index("core")
    pl.when(core == 0)(lambda: place(across, inside))
    pl.when(core == 1)(lambda: place(inside, across))
    lane = iota((1, 128), 1)
    low = lane < 64

    for z in range(-5, 13):
        def plane(c):
            if z < 0:
                return before[c * DEEP + z + 5]
            if z >= 8:
                return behind[c * DEEP + z - 8]
            return vol[c, z]
        v = jnp.concatenate([plane(c).astype(F32) for c in range(C_IN)], axis=0)
        stack = jnp.concatenate(taps(v, 128), axis=0).astype(BF16)
        for kd in range(3):
            to = z - kd + 1 + 4
            if 0 <= to < 16:
                p1[kd * 96 : (kd + 1) * 96, to * 128 : (to + 1) * 128] = stack
    p1[288:, :] = jnp.ones((96, 2048), BF16)

    pooled = []
    for d in range(8):
        pre = dot(t1[...], p1[:, d * 256 : (d + 1) * 256])
        if 2 <= d < 6:
            pre1[:, (d - 2) * 256 : (d - 1) * 256] = pre
        act = leaky(pre).reshape(4, 2, C_MID, 256)
        act = (act[:, 0] + act[:, 1]).reshape(128, 256)
        pooled.append(paired(act[:, :128] + act[:, 128:]))

    row, col = iota((256, 128), 0), iota((256, 128), 1)
    pool = jnp.where((row // 128 == col // 64) & (row % 128 == col % 64 * 2), 1.0, 0.0).astype(BF16)
    m_before = before[ONES_AT].astype(F32)[:1]
    m_behind = behind[ONES_AT].astype(F32)[:1]
    pairs = [jnp.concatenate([pooled[r], pooled[r + 2]], axis=1) for r in range(6)]
    chosen = dot(jnp.concatenate(pairs, axis=0), pool)
    for r in range(6):
        act = chosen[r * 128 : (r + 1) * 128]
        if r < 2:
            act = act * jnp.where(low, m_before, 1.0)
        if r >= 4:
            act = act * jnp.where(low, 1.0, m_behind)
        stack = jnp.concatenate(taps(act, 64), axis=0).astype(BF16)
        for kd in range(3):
            to = r - kd
            if 0 <= to < 4:
                p2[kd * 384 : (kd + 1) * 384, to * 128 : (to + 1) * 128] = stack
    p2[1152:, :] = jnp.ones((128, 512), BF16)

    pre2 = dot(t2[...], p2[...])

    act = leaky(pre2[:, 128:384]).reshape(2, 2, C_OUT, 256)
    act = act[:, 0] + act[:, 1]
    act = act[:, :, :128] + act[:, :, 128:]
    row, col = iota((64, 128), 0), iota((64, 128), 1)
    pool = jnp.where((row // 32 == col // 64) & (row % 32 * 2 == col % 64), 1.0, 0.0).astype(BF16)
    for y in range(2):
        out = dot(pool, paired(act[y]), ((1,), (1,)))
        for d in range(2):
            feat[d, y] = out[d * 32 : (d + 1) * 32].astype(BF16)

    pieces = [before[COT_AT:ONES_AT].astype(F32).reshape(32, 128)]
    for d in range(2):
        pieces.append(jnp.concatenate([cot[d, 0].astype(F32), cot[d, 1].astype(F32)], axis=1))
    pieces.append(behind[COT_AT:ONES_AT].astype(F32).reshape(32, 128))
    cots = jnp.concatenate(pieces, axis=0).T.astype(BF16)
    row, col = iota((128, 384), 0), iota((128, 384), 1)
    spread = jnp.where((row // 32 == col // 128 + col % 128 // 64) & (row % 32 == col % 64 // 2), 0.125, 0.0)
    up = dot(cots, spread.astype(BF16))
    up = jnp.concatenate([up[:, :256], up[:, 128:]], axis=1).reshape(2, 1, C_OUT, 512)
    mask = pre2.reshape(2, 2, C_OUT, 512) > 0.0
    grad = jnp.where(mask, up, 0.3 * up).reshape(256, 512).astype(BF16)
    for r in range(4):
        piece = grad[:, r * 128 : (r + 1) * 128].astype(F32)
        for kx, tap in enumerate(reversed(taps(piece, 64))):
            g4x[kx * 256 : (kx + 1) * 256, r * 128 : (r + 1) * 128] = tap.astype(BF16)

    early = dot(t2g[128:384], g4x[:, 0:256])
    late = dot(t2g[0:256], g4x[:, 256:512])
    back = jnp.concatenate([early[:128, 128:] + early[128:, :128], early[128:, 128:] + late[128:, :128]], axis=1)
    back = back + late[:128]
    one = back * 0.125
    less = 0.3 * one
    stack = jnp.concatenate([one[:, :128], one[:, 128:], less[:, :128], less[:, 128:]], axis=0)
    row, col = iota((128, 256), 0), iota((128, 256), 1)
    spread = jnp.where(row == col // 128 * 64 + col % 128 // 2, 1.0, 0.0).astype(BF16)
    wide = dot(stack.astype(BF16), spread)
    for z in range(8):
        a = z // 2
        at, half = (a % 2) * 128, (a // 2) * 128
        yes = wide[at : at + 128, half : half + 128].reshape(4, 1, C_MID, 128)
        no = wide[256 + at : 384 + at, half : half + 128].reshape(4, 1, C_MID, 128)
        mask = pre1[:, z * 128 : (z + 1) * 128].reshape(4, 2, C_MID, 128) > 0.0
        g1[:, z * 128 : (z + 1) * 128] = jnp.where(mask, yes, no).reshape(256, 128).astype(BF16)

    d2 = dot(p2[0:1168, 128:384], g4x[256:512, 128:384], ((1,), (1,)))
    for kd in range(3):
        for kx in range(3):
            base = (kd * 3 + kx) * 128
            def block(y, p):
                return d2[base + y * 32 : base + (y + 1) * 32, p * 128 : (p + 1) * 128]
            for ky in range(3):
                even = [block(y, p) for p in range(2) for y in [2 * p + ky - 1] if 0 <= y < 4]
                odd = [block(y, p) for p in range(2) for y in [2 * p + ky] if 0 <= y < 4]
                total = sum(even[1:], even[0]) + rolled(sum(odd[1:], odd[0]), 64)
                at = ROWS_W2 + ((kd * 3 + ky) * 3 + kx) * 16
                grads[at : at + 16] = jnp.where(low, total[:16], rolled(total[16:], 64)).astype(BF16)
    scale = bias_scale()
    bias = d2[1152:1168, :128] + d2[1152:1168, 128:]
    grads[ROWS_B2 : ROWS_B2 + 16] = ((bias + rolled(bias, 64)) * scale).astype(BF16)

    d1 = dot(p1[0:304, 512:1536], g1[...], ((1,), (1,)))
    body = d1[:288].reshape(36, 8, 256)
    ky = iota((1, 8, 256), 1) - iota((1, 8, 256), 2) // C_MID + 1
    total = jnp.zeros((36, 128), F32)
    for k in range(3):
        part = jnp.sum(jnp.where(ky == k, body, 0.0), axis=1)
        part = part[:, :128] + part[:, 128:]
        part = part + rolled(part, 64)
        part = part + rolled(part, 32)
        total = jnp.where(lane // 32 == k, part, total)
    total = jnp.concatenate([total, jnp.zeros((12, 128), F32)], axis=0)
    grads[ROWS_W1 : ROWS_W1 + 48] = total.astype(BF16)
    bias = d1[288:304, :128] + d1[288:304, 128:]
    bias = bias + rolled(bias, 64)
    grads[ROWS_B1 : ROWS_B1 + 16] = ((bias + rolled(bias, 32)) * scale).astype(BF16)


def unpack_kernel(grads, w1, b1, w2, b2):
    for t in range(27):
        block = grads[t * 16 : (t + 1) * 16].astype(F32)
        w2[t, 0:16] = block[:, :64]
        w2[t, 16:32] = rolled(block, 64)[:, :64]
    body = grads[ROWS_W1 : ROWS_W1 + 48].astype(F32)
    for ky in range(3):
        part = rolled(body, (128 - 32 * ky) % 128) if ky else body
        for kd in range(3):
            for kx in range(3):
                at = (kd * 3 + kx) * C_IN
                w1[(kd * 3 + ky) * 3 + kx] = part[at : at + C_IN, :C_MID]
    weigh = 1.0 / (16.0 * bias_scale())
    body = grads[ROWS_B2 : ROWS_B2 + 16].astype(F32) * weigh
    b2[...] = jnp.sum(body, axis=0, keepdims=True)[:, :C_OUT]
    body = grads[ROWS_B1 : ROWS_B1 + 16].astype(F32) * weigh
    b1[...] = jnp.sum(body, axis=0, keepdims=True)[:, :C_MID]


def call(kernel, outs, *args, scratch=(), place=pltpu.VMEM):
    return pl.pallas_call(
        kernel,
        out_shape=[jax.ShapeDtypeStruct(s, t) for s, t in outs],
        in_specs=[pl.BlockSpec(memory_space=place)] * len(args),
        out_specs=[VMEM] * len(outs),
        scratch_shapes=scratch,
        compiler_params=PARAMS,
    )(*args)


def sum_kernel(pieces, out):
    total = pieces[0].astype(F32)
    for i in range(1, pieces.shape[0]):
        total = total + pieces[i].astype(F32)
    total = total.astype(BF16)
    for i in range(out.shape[0]):
        out[i] = total


def summed_over_devices(grads):
    near = ("y", "x", "core")
    count, far = lax.axis_size(near), lax.axis_size("z")
    rows = ROWS // count
    pieces = lax.all_to_all(grads.reshape(count, rows, 128), near, 0, 0)
    (mine,) = call(sum_kernel, [((far, rows, 128), BF16)], pieces)
    pieces = lax.all_to_all(mine, "z", 0, 0)
    (mine,) = call(sum_kernel, [((count, rows, 128), BF16)], pieces)
    return lax.all_to_all(mine, near, 0, 0).reshape(ROWS, 128)


def local(volume, w_first, b_first, w_second, b_second, cotangent):
    cot = jnp.transpose(cotangent[0], (1, 2, 3, 0))
    w1 = jnp.transpose(w_first, (2, 3, 4, 1, 0)).reshape(27, C_IN, C_MID)
    w2 = jnp.transpose(w_second, (2, 3, 4, 1, 0)).reshape(27, C_MID, C_OUT)
    args = [pltpu.with_memory_space_constraint(a, pltpu.HBM) for a in (volume[0], cot, w1, b_first, w2, b_second)]
    inside, across, vol, cot, w1, b1, w2, b2 = call(
        pack_kernel,
        [((BLOCKS, 8, 128), BF16)] * 2 + [(a.shape, a.dtype) for a in args],
        *args,
        scratch=[pltpu.SemaphoreType.DMA((len(args),))],
        place=pltpu.HBM,
    )
    space = ("x", "core")
    count = lax.axis_size(space)
    pairs = [(i, i + 1) for i in range(0, count, 2)]
    inside = lax.ppermute(inside, space, pairs + [(j, i) for i, j in pairs])
    pairs = [(i, i + 1) for i in range(1, count - 1, 2)]
    across = lax.ppermute(across, space, pairs + [(j, i) for i, j in pairs])
    t1, t2, t2g = call(
        weights_kernel,
        [((256, 384), BF16), ((256, 1280), BF16), ((384, 768), BF16)],
        w1, b1, w2, b2,
    )
    feat, grads = call(
        main_kernel,
        [((2, 2, 32, C_OUT), BF16), ((ROWS, 128), BF16)],
        vol, inside, across, cot, t1, t2, t2g,
        scratch=[
            pltpu.VMEM((BLOCKS, 8, 128), BF16),
            pltpu.VMEM((BLOCKS, 8, 128), BF16),
            pltpu.VMEM((384, 2048), BF16),
            pltpu.VMEM((256, 1024), F32),
            pltpu.VMEM((1280, 512), BF16),
            pltpu.VMEM((768, 512), BF16),
            pltpu.VMEM((256, 1024), BF16),
        ],
    )
    grads = summed_over_devices(grads)
    gw1, gb1, gw2, gb2 = call(
        unpack_kernel,
        [((27, C_IN, C_MID), F32), ((1, C_MID), F32), ((27, C_MID, C_OUT), F32), ((1, C_OUT), F32)],
        grads,
    )
    gw1 = jnp.transpose(gw1.reshape(3, 3, 3, C_IN, C_MID), (4, 3, 0, 1, 2))
    gw2 = jnp.transpose(gw2.reshape(3, 3, 3, C_MID, C_OUT), (4, 3, 0, 1, 2))
    return jnp.transpose(feat, (3, 0, 1, 2))[None], gw1, gb1[0], gw2, gb2[0]


def solution(mesh):
    dp, space = mesh.devices.shape
    y = 4 if dp % 4 == 0 else 1
    grid = Mesh(mesh.devices.reshape(dp // y, y, space // 2, 2), ("z", "y", "x", "core"))
    data = P(("z", "y"), None, ("x", "core"), None, None)
    return jax.shard_map(
        local,
        mesh=grid,
        in_specs=(data, P(), P(), P(), P(), data),
        out_specs=(data, P(), P(), P(), P()),
        check_vma=False,
    )
```

```python
import jax
import jax.numpy as jnp
from jax import lax
from jax.experimental import pallas as pl
from jax.experimental.pallas import tpu as pltpu
from jax.sharding import Mesh, PartitionSpec as P

BF16, F32 = jnp.bfloat16, jnp.float32
VMEM = pl.BlockSpec(memory_space=pltpu.VMEM)
PARAMS = pltpu.CompilerParams(vmem_limit_bytes=48 * 1024 * 1024)
C_IN, C_MID, C_OUT, Y, X = 4, 32, 64, 8, 128
DEEP = 5
COT_AT = C_IN * DEEP
ONES_AT = COT_AT + 4
BLOCKS = ONES_AT + 1
ROWS_W2, ROWS_W1, ROWS_B2, ROWS_B1, ROWS = 0, 432, 480, 496, 512


def dot(a, b, dims=((1,), (0,))):
    return lax.dot_general(a, b, (dims, ((), ())), preferred_element_type=F32)


def iota(shape, dim):
    return lax.broadcasted_iota(jnp.int32, shape, dim)


def leaky(v):
    return jnp.maximum(v, 0.3 * v)


def rolled(v, shift):
    return pltpu.roll(v, shift, 1)


def paired(v):
    return ((v + rolled(v, v.shape[1] - 1)) * 0.125).astype(BF16)


def bias_scale():
    return 1.0 + iota((16, 128), 0).astype(F32) * 0.0625


def taps(v, period):
    place = iota(v.shape, 1) % period
    before = jnp.where(place == 0, 0.0, rolled(v, 1))
    after = jnp.where(place == period - 1, 0.0, rolled(v, v.shape[1] - 1))
    return before, v, after


def pack_kernel(vol_at, cot_at, w1_at, b1_at, w2_at, b2_at, across, inside, vol, cot, w1, b1, w2, b2, sems):
    pairs = ((vol_at, vol), (cot_at, cot), (w1_at, w1), (b1_at, b1), (w2_at, w2), (b2_at, b2))
    copies = [pltpu.make_async_copy(a, b, sems.at[i]) for i, (a, b) in enumerate(pairs)]
    for copy in copies:
        copy.start()
    across[ONES_AT] = jnp.ones((8, 128), BF16)
    inside[ONES_AT] = jnp.ones((8, 128), BF16)
    copies[0].wait()
    copies[1].wait()

    def fill(first, last):
        for c in range(C_IN):
            first[c * DEEP : (c + 1) * DEEP] = vol[c, :DEEP]
            last[c * DEEP : (c + 1) * DEEP] = vol[c, 8 - DEEP :]
        for ref, d in ((first, 0), (last, 1)):
            both = jnp.concatenate([cot[d, 0].astype(F32), cot[d, 1].astype(F32)], axis=1)
            ref[COT_AT:ONES_AT] = both.reshape(4, 8, 128).astype(BF16)

    core = lax.axis_index("core")
    pl.when(core == 0)(lambda: fill(across, inside))
    pl.when(core == 1)(lambda: fill(inside, across))
    for copy in copies[2:]:
        copy.wait()


def bias_rows(bias, copies):
    hi = bias.astype(BF16).astype(F32)
    lo = (bias - hi).astype(BF16).astype(F32)
    rest = bias - hi - lo
    hi, lo, rest = (jnp.concatenate([v] * copies, axis=1) for v in (hi, lo, rest))
    row = iota((128, 256), 0)
    zero = jnp.zeros((128, 256), F32)
    return jnp.where(row == 0, hi, jnp.where(row == 1, lo, jnp.where(row == 2, rest, zero)))


def weights_kernel(w1, b1, w2, b2, t1, t2, t2g):
    narrow = jnp.concatenate([w1[t].astype(F32) for t in range(27)], axis=0)
    wide = jnp.concatenate([narrow] * 4, axis=1)
    y_in = iota((8, 128), 0)
    lanes = iota((8, 128), 1) // C_MID
    blocks = []
    for kd in range(3):
        for kx in range(3):
            for c in range(C_IN):
                halves = []
                for half in range(2):
                    ky = y_in - (lanes + 4 * half) + 1
                    total = jnp.zeros((8, 128), F32)
                    for k in range(3):
                        at = ((kd * 3 + k) * 3 + kx) * C_IN + c
                        total = jnp.where(ky == k, wide[at : at + 1], total)
                    halves.append(total)
                blocks.append(jnp.concatenate(halves, axis=1))
    body = jnp.concatenate(blocks + [bias_rows(b1[...].reshape(1, C_MID), 8)[:96]], axis=0)
    t1[...] = body.T.astype(BF16)
    nothing = jnp.zeros((C_MID, C_OUT), F32)
    for kd in range(3):
        for kx in range(3):
            w = [w2[(kd * 3 + ky) * 3 + kx].astype(F32) for ky in range(3)]
            pair = {
                a: jnp.concatenate([w[a] if a < 3 else nothing, w[a - 1] if a > 0 else nothing], axis=1)
                for a in range(4)
            }
            none = jnp.zeros((C_MID, 128), F32)
            block = jnp.concatenate(
                [
                    jnp.concatenate([pair.get(y - 2 * p + 1, none) for p in range(2)], axis=1)
                    for y in range(4)
                ],
                axis=0,
            )
            t2g[kd * 128 : (kd + 1) * 128, kx * 256 : (kx + 1) * 256] = block.astype(BF16)
            at = (kd * 3 + kx) * 128
            t2[:, at : at + 128] = block.T.astype(BF16)
    t2[:, 1152:] = bias_rows(b2[...].reshape(1, C_OUT), 4).T.astype(BF16)


def main_kernel(vol, across, inside, cot, t1, t2, t2g, feat, grads, before, behind, p1, pre1, p2, g4x, g1):
    def place(first, second):
        before[...] = first[...]
        behind[...] = second[...]

    core = lax.axis_index("core")
    pl.when(core == 0)(lambda: place(across, inside))
    pl.when(core == 1)(lambda: place(inside, across))
    lane = iota((1, 128), 1)
    low = lane < 64

    for z in range(-5, 13):
        def plane(c):
            if z < 0:
                return before[c * DEEP + z + 5]
            if z >= 8:
                return behind[c * DEEP + z - 8]
            return vol[c, z]
        v = jnp.concatenate([plane(c).astype(F32) for c in range(C_IN)], axis=0)
        stack = jnp.concatenate(taps(v, 128), axis=0).astype(BF16)
        for kd in range(3):
            to = z - kd + 1 + 4
            if 0 <= to < 16:
                p1[kd * 96 : (kd + 1) * 96, to * 128 : (to + 1) * 128] = stack
    p1[288:, :] = jnp.ones((96, 2048), BF16)

    pooled = []
    for d in range(8):
        pre = dot(t1[...], p1[:, d * 256 : (d + 1) * 256])
        if 2 <= d < 6:
            pre1[:, (d - 2) * 256 : (d - 1) * 256] = pre
        act = leaky(pre).reshape(4, 2, C_MID, 256)
        act = (act[:, 0] + act[:, 1]).reshape(128, 256)
        pooled.append(paired(act[:, :128] + act[:, 128:]))

    row, col = iota((256, 128), 0), iota((256, 128), 1)
    pool = jnp.where((row // 128 == col // 64) & (row % 128 == col % 64 * 2), 1.0, 0.0).astype(BF16)
    m_before = before[ONES_AT].astype(F32)[:1]
    m_behind = behind[ONES_AT].astype(F32)[:1]
    pairs = [jnp.concatenate([pooled[r], pooled[r + 2]], axis=1) for r in range(6)]
    chosen = dot(jnp.concatenate(pairs, axis=0), pool)
    for r in range(6):
        act = chosen[r * 128 : (r + 1) * 128]
        if r < 2:
            act = act * jnp.where(low, m_before, 1.0)
        if r >= 4:
            act = act * jnp.where(low, 1.0, m_behind)
        stack = jnp.concatenate(taps(act, 64), axis=0).astype(BF16)
        for kd in range(3):
            to = r - kd
            if 0 <= to < 4:
                p2[kd * 384 : (kd + 1) * 384, to * 128 : (to + 1) * 128] = stack
    p2[1152:, :] = jnp.ones((128, 512), BF16)

    pre2 = dot(t2[...], p2[...])

    act = leaky(pre2[:, 128:384]).reshape(2, 2, C_OUT, 256)
    act = act[:, 0] + act[:, 1]
    act = act[:, :, :128] + act[:, :, 128:]
    row, col = iota((64, 128), 0), iota((64, 128), 1)
    pool = jnp.where((row // 32 == col // 64) & (row % 32 * 2 == col % 64), 1.0, 0.0).astype(BF16)
    for y in range(2):
        out = dot(pool, paired(act[y]), ((1,), (1,)))
        for d in range(2):
            feat[d, y] = out[d * 32 : (d + 1) * 32].astype(BF16)

    pieces = [before[COT_AT:ONES_AT].astype(F32).reshape(32, 128)]
    for d in range(2):
        pieces.append(jnp.concatenate([cot[d, 0].astype(F32), cot[d, 1].astype(F32)], axis=1))
    pieces.append(behind[COT_AT:ONES_AT].astype(F32).reshape(32, 128))
    cots = jnp.concatenate(pieces, axis=0).T.astype(BF16)
    row, col = iota((128, 384), 0), iota((128, 384), 1)
    spread = jnp.where((row // 32 == col // 128 + col % 128 // 64) & (row % 32 == col % 64 // 2), 0.125, 0.0)
    up = dot(cots, spread.astype(BF16))
    up = jnp.concatenate([up[:, :256], up[:, 128:]], axis=1).reshape(2, 1, C_OUT, 512)
    mask = pre2.reshape(2, 2, C_OUT, 512) > 0.0
    grad = jnp.where(mask, up, 0.3 * up).reshape(256, 512).astype(BF16)
    for r in range(4):
        piece = grad[:, r * 128 : (r + 1) * 128].astype(F32)
        for kx, tap in enumerate(reversed(taps(piece, 64))):
            g4x[kx * 256 : (kx + 1) * 256, r * 128 : (r + 1) * 128] = tap.astype(BF16)

    early = dot(t2g[128:384], g4x[:, 0:256])
    late = dot(t2g[0:256], g4x[:, 256:512])
    back = jnp.concatenate([early[:128, 128:] + early[128:, :128], early[128:, 128:] + late[128:, :128]], axis=1)
    back = back + late[:128]
    one = back * 0.125
    less = 0.3 * one
    stack = jnp.concatenate([one[:, :128], one[:, 128:], less[:, :128], less[:, 128:]], axis=0)
    row, col = iota((128, 256), 0), iota((128, 256), 1)
    spread = jnp.where(row == col // 128 * 64 + col % 128 // 2, 1.0, 0.0).astype(BF16)
    wide = dot(stack.astype(BF16), spread)
    for z in range(8):
        a = z // 2
        at, half = (a % 2) * 128, (a // 2) * 128
        yes = wide[at : at + 128, half : half + 128].reshape(4, 1, C_MID, 128)
        no = wide[256 + at : 384 + at, half : half + 128].reshape(4, 1, C_MID, 128)
        mask = pre1[:, z * 128 : (z + 1) * 128].reshape(4, 2, C_MID, 128) > 0.0
        g1[:, z * 128 : (z + 1) * 128] = jnp.where(mask, yes, no).reshape(256, 128).astype(BF16)

    d2 = dot(p2[0:1168, 128:384], g4x[256:512, 128:384], ((1,), (1,)))
    for kd in range(3):
        for kx in range(3):
            base = (kd * 3 + kx) * 128
            def block(y, p):
                return d2[base + y * 32 : base + (y + 1) * 32, p * 128 : (p + 1) * 128]
            for ky in range(3):
                even = [block(y, p) for p in range(2) for y in [2 * p + ky - 1] if 0 <= y < 4]
                odd = [block(y, p) for p in range(2) for y in [2 * p + ky] if 0 <= y < 4]
                total = sum(even[1:], even[0]) + rolled(sum(odd[1:], odd[0]), 64)
                at = ROWS_W2 + ((kd * 3 + ky) * 3 + kx) * 16
                grads[at : at + 16] = jnp.where(low, total[:16], rolled(total[16:], 64)).astype(BF16)
    scale = bias_scale()
    bias = d2[1152:1168, :128] + d2[1152:1168, 128:]
    grads[ROWS_B2 : ROWS_B2 + 16] = ((bias + rolled(bias, 64)) * scale).astype(BF16)

    d1 = dot(p1[0:304, 512:1536], g1[...], ((1,), (1,)))
    body = d1[:288].reshape(36, 8, 256)
    ky = iota((1, 8, 256), 1) - iota((1, 8, 256), 2) // C_MID + 1
    total = jnp.zeros((36, 128), F32)
    for k in range(3):
        part = jnp.sum(jnp.where(ky == k, body, 0.0), axis=1)
        part = part[:, :128] + part[:, 128:]
        part = part + rolled(part, 64)
        part = part + rolled(part, 32)
        total = jnp.where(lane // 32 == k, part, total)
    total = jnp.concatenate([total, jnp.zeros((12, 128), F32)], axis=0)
    grads[ROWS_W1 : ROWS_W1 + 48] = total.astype(BF16)
    bias = d1[288:304, :128] + d1[288:304, 128:]
    bias = bias + rolled(bias, 64)
    grads[ROWS_B1 : ROWS_B1 + 16] = ((bias + rolled(bias, 32)) * scale).astype(BF16)


def unpack_kernel(grads, w1, b1, w2, b2):
    for t in range(27):
        block = grads[t * 16 : (t + 1) * 16].astype(F32)
        w2[t, 0:16] = block[:, :64]
        w2[t, 16:32] = rolled(block, 64)[:, :64]
    body = grads[ROWS_W1 : ROWS_W1 + 48].astype(F32)
    for ky in range(3):
        part = rolled(body, (128 - 32 * ky) % 128) if ky else body
        for kd in range(3):
            for kx in range(3):
                at = (kd * 3 + kx) * C_IN
                w1[(kd * 3 + ky) * 3 + kx] = part[at : at + C_IN, :C_MID]
    weigh = 1.0 / (16.0 * bias_scale())
    body = grads[ROWS_B2 : ROWS_B2 + 16].astype(F32) * weigh
    b2[...] = jnp.sum(body, axis=0, keepdims=True)[:, :C_OUT]
    body = grads[ROWS_B1 : ROWS_B1 + 16].astype(F32) * weigh
    b1[...] = jnp.sum(body, axis=0, keepdims=True)[:, :C_MID]


def call(kernel, outs, *args, scratch=(), place=pltpu.VMEM):
    return pl.pallas_call(
        kernel,
        out_shape=[jax.ShapeDtypeStruct(s, t) for s, t in outs],
        in_specs=[pl.BlockSpec(memory_space=place)] * len(args),
        out_specs=[VMEM] * len(outs),
        scratch_shapes=scratch,
        compiler_params=PARAMS,
    )(*args)


def sum_kernel(pieces, out):
    total = pieces[0].astype(F32)
    for i in range(1, pieces.shape[0]):
        total = total + pieces[i].astype(F32)
    total = total.astype(BF16)
    for i in range(out.shape[0]):
        out[i] = total


def rounded(count, first):
    return [[(first + i) % count for i in range(count)]]


def summed_over_devices(grads):
    near = ("y", "x", "core")
    y, x, core = (lax.axis_size(axis) for axis in near)
    count, far = y * x * core, lax.axis_size("z")
    plane = rounded(count, (y // 2 * x + x // 2) * core)
    line = rounded(far, far // 2)
    rows = ROWS // count
    pieces = lax.all_to_all(grads.reshape(count, rows, 128), near, 0, 0, axis_index_groups=plane)
    (mine,) = call(sum_kernel, [((far, rows, 128), BF16)], pieces)
    pieces = lax.all_to_all(mine, "z", 0, 0, axis_index_groups=line)
    (mine,) = call(sum_kernel, [((count, rows, 128), BF16)], pieces)
    return lax.all_to_all(mine, near, 0, 0, axis_index_groups=plane).reshape(ROWS, 128)


def local(volume, w_first, b_first, w_second, b_second, cotangent):
    cot = jnp.transpose(cotangent[0], (1, 2, 3, 0))
    w1 = jnp.transpose(w_first, (2, 3, 4, 1, 0)).reshape(27, C_IN, C_MID)
    w2 = jnp.transpose(w_second, (2, 3, 4, 1, 0)).reshape(27, C_MID, C_OUT)
    args = [pltpu.with_memory_space_constraint(a, pltpu.HBM) for a in (volume[0], cot, w1, b_first, w2, b_second)]
    across, inside, vol, cot, w1, b1, w2, b2 = call(
        pack_kernel,
        [((BLOCKS, 8, 128), BF16)] * 2 + [(a.shape, a.dtype) for a in args],
        *args,
        scratch=[pltpu.SemaphoreType.DMA((len(args),))],
        place=pltpu.HBM,
    )
    space = ("x", "core")
    count = lax.axis_size(space)
    pairs = [(i, i + 1) for i in range(0, count, 2)]
    inside = lax.ppermute(inside, space, pairs + [(j, i) for i, j in pairs])
    pairs = [(i, i + 1) for i in range(1, count - 1, 2)]
    across = lax.ppermute(across, space, pairs + [(j, i) for i, j in pairs])
    t1, t2, t2g = call(
        weights_kernel,
        [((256, 384), BF16), ((256, 1280), BF16), ((384, 768), BF16)],
        w1, b1, w2, b2,
    )
    feat, grads = call(
        main_kernel,
        [((2, 2, 32, C_OUT), BF16), ((ROWS, 128), BF16)],
        vol, across, inside, cot, t1, t2, t2g,
        scratch=[
            pltpu.VMEM((BLOCKS, 8, 128), BF16),
            pltpu.VMEM((BLOCKS, 8, 128), BF16),
            pltpu.VMEM((384, 2048), BF16),
            pltpu.VMEM((256, 1024), F32),
            pltpu.VMEM((1280, 512), BF16),
            pltpu.VMEM((768, 512), BF16),
            pltpu.VMEM((256, 1024), BF16),
        ],
    )
    grads = summed_over_devices(grads)
    gw1, gb1, gw2, gb2 = call(
        unpack_kernel,
        [((27, C_IN, C_MID), F32), ((1, C_MID), F32), ((27, C_MID, C_OUT), F32), ((1, C_OUT), F32)],
        grads,
    )
    gw1 = jnp.transpose(gw1.reshape(3, 3, 3, C_IN, C_MID), (4, 3, 0, 1, 2))
    gw2 = jnp.transpose(gw2.reshape(3, 3, 3, C_MID, C_OUT), (4, 3, 0, 1, 2))
    return jnp.transpose(feat, (3, 0, 1, 2))[None], gw1, gb1[0], gw2, gb2[0]


def solution(mesh):
    dp, space = mesh.devices.shape
    y = 4 if dp % 4 == 0 else 1
    grid = Mesh(mesh.devices.reshape(dp // y, y, space // 2, 2), ("z", "y", "x", "core"))
    data = P(("z", "y"), None, ("x", "core"), None, None)
    return jax.shard_map(
        local,
        mesh=grid,
        in_specs=(data, P(), P(), P(), P(), data),
        out_specs=(data, P(), P(), P(), P()),
        check_vma=False,
    )
```

```python
import jax
import jax.numpy as jnp
from jax import lax
from jax.experimental import pallas as pl
from jax.experimental.pallas import tpu as pltpu
from jax.sharding import Mesh, PartitionSpec as P

BF16, F32 = jnp.bfloat16, jnp.float32
VMEM = pl.BlockSpec(memory_space=pltpu.VMEM)
PARAMS = pltpu.CompilerParams(vmem_limit_bytes=48 * 1024 * 1024)
C_IN, C_MID, C_OUT, Y, X = 4, 32, 64, 8, 128
DEEP = 5
COT_AT = C_IN * DEEP
ONES_AT = COT_AT + 4
BLOCKS = ONES_AT + 1
ROWS_W2, ROWS_W1, ROWS_B2, ROWS_B1, ROWS = 0, 432, 480, 496, 512


def dot(a, b, dims=((1,), (0,))):
    return lax.dot_general(a, b, (dims, ((), ())), preferred_element_type=F32)


def iota(shape, dim):
    return lax.broadcasted_iota(jnp.int32, shape, dim)


def leaky(v):
    return jnp.maximum(v, 0.3 * v)


def rolled(v, shift):
    return pltpu.roll(v, shift, 1)


def paired(v):
    return ((v + rolled(v, v.shape[1] - 1)) * 0.125).astype(BF16)


def bias_scale():
    return 1.0 + iota((16, 128), 0).astype(F32) * 0.0625


def taps(v, period):
    place = iota(v.shape, 1) % period
    before = jnp.where(place == 0, 0.0, rolled(v, 1))
    after = jnp.where(place == period - 1, 0.0, rolled(v, v.shape[1] - 1))
    return before, v, after


def pack_kernel(vol_at, cot_at, w1_at, b1_at, w2_at, b2_at, across, inside, vol, cot, w1, b1, w2, b2, sems):
    pairs = ((vol_at, vol), (cot_at, cot), (w1_at, w1), (b1_at, b1), (w2_at, w2), (b2_at, b2))
    copies = [pltpu.make_async_copy(a, b, sems.at[i]) for i, (a, b) in enumerate(pairs)]
    for copy in copies:
        copy.start()
    across[ONES_AT] = jnp.ones((8, 128), BF16)
    inside[ONES_AT] = jnp.ones((8, 128), BF16)
    copies[0].wait()
    copies[1].wait()

    def fill(first, last):
        for c in range(C_IN):
            first[c * DEEP : (c + 1) * DEEP] = vol[c, :DEEP]
            last[c * DEEP : (c + 1) * DEEP] = vol[c, 8 - DEEP :]
        for ref, d in ((first, 0), (last, 1)):
            both = jnp.concatenate([cot[d, 0].astype(F32), cot[d, 1].astype(F32)], axis=1)
            ref[COT_AT:ONES_AT] = both.reshape(4, 8, 128).astype(BF16)

    core = lax.axis_index("core")
    pl.when(core == 0)(lambda: fill(across, inside))
    pl.when(core == 1)(lambda: fill(inside, across))
    for copy in copies[2:]:
        copy.wait()


def bias_rows(bias, copies):
    hi = bias.astype(BF16).astype(F32)
    lo = (bias - hi).astype(BF16).astype(F32)
    rest = bias - hi - lo
    hi, lo, rest = (jnp.concatenate([v] * copies, axis=1) for v in (hi, lo, rest))
    row = iota((128, 256), 0)
    zero = jnp.zeros((128, 256), F32)
    return jnp.where(row == 0, hi, jnp.where(row == 1, lo, jnp.where(row == 2, rest, zero)))


def weights_kernel(w1, b1, w2, b2, t1, t2, t2g):
    narrow = jnp.concatenate([w1[t].astype(F32) for t in range(27)], axis=0)
    wide = jnp.concatenate([narrow] * 4, axis=1)
    y_in = iota((8, 128), 0)
    lanes = iota((8, 128), 1) // C_MID
    blocks = []
    for kd in range(3):
        for kx in range(3):
            for c in range(C_IN):
                halves = []
                for half in range(2):
                    ky = y_in - (lanes + 4 * half) + 1
                    total = jnp.zeros((8, 128), F32)
                    for k in range(3):
                        at = ((kd * 3 + k) * 3 + kx) * C_IN + c
                        total = jnp.where(ky == k, wide[at : at + 1], total)
                    halves.append(total)
                blocks.append(jnp.concatenate(halves, axis=1))
    body = jnp.concatenate(blocks + [bias_rows(b1[...].reshape(1, C_MID), 8)[:96]], axis=0)
    t1[...] = body.T.astype(BF16)
    nothing = jnp.zeros((C_MID, C_OUT), F32)
    for kd in range(3):
        for kx in range(3):
            w = [w2[(kd * 3 + ky) * 3 + kx].astype(F32) for ky in range(3)]
            pair = {
                a: jnp.concatenate([w[a] if a < 3 else nothing, w[a - 1] if a > 0 else nothing], axis=1)
                for a in range(4)
            }
            none = jnp.zeros((C_MID, 128), F32)
            block = jnp.concatenate(
                [
                    jnp.concatenate([pair.get(y - 2 * p + 1, none) for p in range(2)], axis=1)
                    for y in range(4)
                ],
                axis=0,
            )
            t2g[kd * 128 : (kd + 1) * 128, kx * 256 : (kx + 1) * 256] = block.astype(BF16)
            at = (kd * 3 + kx) * 128
            t2[:, at : at + 128] = block.T.astype(BF16)
    t2[:, 1152:] = bias_rows(b2[...].reshape(1, C_OUT), 4).T.astype(BF16)


def main_kernel(vol, across, inside, cot, t1, t2, t2g, feat, grads, before, behind, p1, pre1, p2, g4x, g1):
    def place(first, second):
        before[...] = first[...]
        behind[...] = second[...]

    core = lax.axis_index("core")
    pl.when(core == 0)(lambda: place(across, inside.at[1]))
    pl.when(core == 1)(lambda: place(inside.at[0], across))
    lane = iota((1, 128), 1)
    low = lane < 64

    for z in range(-5, 13):
        def plane(c):
            if z < 0:
                return before[c * DEEP + z + 5]
            if z >= 8:
                return behind[c * DEEP + z - 8]
            return vol[c, z]
        v = jnp.concatenate([plane(c).astype(F32) for c in range(C_IN)], axis=0)
        stack = jnp.concatenate(taps(v, 128), axis=0).astype(BF16)
        for kd in range(3):
            to = z - kd + 1 + 4
            if 0 <= to < 16:
                p1[kd * 96 : (kd + 1) * 96, to * 128 : (to + 1) * 128] = stack
    p1[288:, :] = jnp.ones((96, 2048), BF16)

    pooled = []
    for d in range(8):
        pre = dot(t1[...], p1[:, d * 256 : (d + 1) * 256])
        if 2 <= d < 6:
            pre1[:, (d - 2) * 256 : (d - 1) * 256] = pre
        act = leaky(pre).reshape(4, 2, C_MID, 256)
        act = (act[:, 0] + act[:, 1]).reshape(128, 256)
        pooled.append(paired(act[:, :128] + act[:, 128:]))

    row, col = iota((256, 128), 0), iota((256, 128), 1)
    pool = jnp.where((row // 128 == col // 64) & (row % 128 == col % 64 * 2), 1.0, 0.0).astype(BF16)
    m_before = before[ONES_AT].astype(F32)[:1]
    m_behind = behind[ONES_AT].astype(F32)[:1]
    pairs = [jnp.concatenate([pooled[r], pooled[r + 2]], axis=1) for r in range(6)]
    chosen = dot(jnp.concatenate(pairs, axis=0), pool)
    for r in range(6):
        act = chosen[r * 128 : (r + 1) * 128]
        if r < 2:
            act = act * jnp.where(low, m_before, 1.0)
        if r >= 4:
            act = act * jnp.where(low, 1.0, m_behind)
        stack = jnp.concatenate(taps(act, 64), axis=0).astype(BF16)
        for kd in range(3):
            to = r - kd
            if 0 <= to < 4:
                p2[kd * 384 : (kd + 1) * 384, to * 128 : (to + 1) * 128] = stack
    p2[1152:, :] = jnp.ones((128, 512), BF16)

    pre2 = dot(t2[...], p2[...])

    act = leaky(pre2[:, 128:384]).reshape(2, 2, C_OUT, 256)
    act = act[:, 0] + act[:, 1]
    act = act[:, :, :128] + act[:, :, 128:]
    row, col = iota((64, 128), 0), iota((64, 128), 1)
    pool = jnp.where((row // 32 == col // 64) & (row % 32 * 2 == col % 64), 1.0, 0.0).astype(BF16)
    for y in range(2):
        out = dot(pool, paired(act[y]), ((1,), (1,)))
        for d in range(2):
            feat[d, y] = out[d * 32 : (d + 1) * 32].astype(BF16)

    pieces = [before[COT_AT:ONES_AT].astype(F32).reshape(32, 128)]
    for d in range(2):
        pieces.append(jnp.concatenate([cot[d, 0].astype(F32), cot[d, 1].astype(F32)], axis=1))
    pieces.append(behind[COT_AT:ONES_AT].astype(F32).reshape(32, 128))
    cots = jnp.concatenate(pieces, axis=0).T.astype(BF16)
    row, col = iota((128, 384), 0), iota((128, 384), 1)
    spread = jnp.where((row // 32 == col // 128 + col % 128 // 64) & (row % 32 == col % 64 // 2), 0.125, 0.0)
    up = dot(cots, spread.astype(BF16))
    up = jnp.concatenate([up[:, :256], up[:, 128:]], axis=1).reshape(2, 1, C_OUT, 512)
    mask = pre2.reshape(2, 2, C_OUT, 512) > 0.0
    grad = jnp.where(mask, up, 0.3 * up).reshape(256, 512).astype(BF16)
    for r in range(4):
        piece = grad[:, r * 128 : (r + 1) * 128].astype(F32)
        for kx, tap in enumerate(reversed(taps(piece, 64))):
            g4x[kx * 256 : (kx + 1) * 256, r * 128 : (r + 1) * 128] = tap.astype(BF16)

    early = dot(t2g[128:384], g4x[:, 0:256])
    late = dot(t2g[0:256], g4x[:, 256:512])
    back = jnp.concatenate([early[:128, 128:] + early[128:, :128], early[128:, 128:] + late[128:, :128]], axis=1)
    back = back + late[:128]
    one = back * 0.125
    less = 0.3 * one
    stack = jnp.concatenate([one[:, :128], one[:, 128:], less[:, :128], less[:, 128:]], axis=0)
    row, col = iota((128, 256), 0), iota((128, 256), 1)
    spread = jnp.where(row == col // 128 * 64 + col % 128 // 2, 1.0, 0.0).astype(BF16)
    wide = dot(stack.astype(BF16), spread)
    for z in range(8):
        a = z // 2
        at, half = (a % 2) * 128, (a // 2) * 128
        yes = wide[at : at + 128, half : half + 128].reshape(4, 1, C_MID, 128)
        no = wide[256 + at : 384 + at, half : half + 128].reshape(4, 1, C_MID, 128)
        mask = pre1[:, z * 128 : (z + 1) * 128].reshape(4, 2, C_MID, 128) > 0.0
        g1[:, z * 128 : (z + 1) * 128] = jnp.where(mask, yes, no).reshape(256, 128).astype(BF16)

    d2 = dot(p2[0:1168, 128:384], g4x[256:512, 128:384], ((1,), (1,)))
    for kd in range(3):
        for kx in range(3):
            base = (kd * 3 + kx) * 128
            def block(y, p):
                return d2[base + y * 32 : base + (y + 1) * 32, p * 128 : (p + 1) * 128]
            for ky in range(3):
                even = [block(y, p) for p in range(2) for y in [2 * p + ky - 1] if 0 <= y < 4]
                odd = [block(y, p) for p in range(2) for y in [2 * p + ky] if 0 <= y < 4]
                total = sum(even[1:], even[0]) + rolled(sum(odd[1:], odd[0]), 64)
                at = ROWS_W2 + ((kd * 3 + ky) * 3 + kx) * 16
                grads[at : at + 16] = jnp.where(low, total[:16], rolled(total[16:], 64)).astype(BF16)
    scale = bias_scale()
    bias = d2[1152:1168, :128] + d2[1152:1168, 128:]
    grads[ROWS_B2 : ROWS_B2 + 16] = ((bias + rolled(bias, 64)) * scale).astype(BF16)

    d1 = dot(p1[0:304, 512:1536], g1[...], ((1,), (1,)))
    body = d1[:288].reshape(36, 8, 256)
    ky = iota((1, 8, 256), 1) - iota((1, 8, 256), 2) // C_MID + 1
    total = jnp.zeros((36, 128), F32)
    for k in range(3):
        part = jnp.sum(jnp.where(ky == k, body, 0.0), axis=1)
        part = part[:, :128] + part[:, 128:]
        part = part + rolled(part, 64)
        part = part + rolled(part, 32)
        total = jnp.where(lane // 32 == k, part, total)
    total = jnp.concatenate([total, jnp.zeros((12, 128), F32)], axis=0)
    grads[ROWS_W1 : ROWS_W1 + 48] = total.astype(BF16)
    bias = d1[288:304, :128] + d1[288:304, 128:]
    bias = bias + rolled(bias, 64)
    grads[ROWS_B1 : ROWS_B1 + 16] = ((bias + rolled(bias, 32)) * scale).astype(BF16)


def unpack_kernel(grads, w1, b1, w2, b2):
    for t in range(27):
        block = grads[t * 16 : (t + 1) * 16].astype(F32)
        w2[t, 0:16] = block[:, :64]
        w2[t, 16:32] = rolled(block, 64)[:, :64]
    body = grads[ROWS_W1 : ROWS_W1 + 48].astype(F32)
    for ky in range(3):
        part = rolled(body, (128 - 32 * ky) % 128) if ky else body
        for kd in range(3):
            for kx in range(3):
                at = (kd * 3 + kx) * C_IN
                w1[(kd * 3 + ky) * 3 + kx] = part[at : at + C_IN, :C_MID]
    weigh = 1.0 / (16.0 * bias_scale())
    body = grads[ROWS_B2 : ROWS_B2 + 16].astype(F32) * weigh
    b2[...] = jnp.sum(body, axis=0, keepdims=True)[:, :C_OUT]
    body = grads[ROWS_B1 : ROWS_B1 + 16].astype(F32) * weigh
    b1[...] = jnp.sum(body, axis=0, keepdims=True)[:, :C_MID]


def call(kernel, outs, *args, scratch=(), place=pltpu.VMEM):
    return pl.pallas_call(
        kernel,
        out_shape=[jax.ShapeDtypeStruct(s, t) for s, t in outs],
        in_specs=[pl.BlockSpec(memory_space=place)] * len(args),
        out_specs=[VMEM] * len(outs),
        scratch_shapes=scratch,
        compiler_params=PARAMS,
    )(*args)


def sum_kernel(pieces, out):
    total = pieces[0].astype(F32)
    for i in range(1, pieces.shape[0]):
        total = total + pieces[i].astype(F32)
    total = total.astype(BF16)
    for i in range(out.shape[0]):
        out[i] = total


def rounded(count, first):
    return [[(first + i) % count for i in range(count)]]


def farthest(count, first):
    return [sorted(range(count), key=lambda i: (i != first, -min((i - first) % count, (first - i) % count)))]


def summed_over_devices(grads):
    near = ("y", "x", "core")
    y, x, core = (lax.axis_size(axis) for axis in near)
    count, far = y * x * core, lax.axis_size("z")
    plane = rounded(count, (y // 2 * x + x // 2) * core + 1)
    line = farthest(far, far // 2)
    rows = ROWS // count
    pieces = lax.all_to_all(grads.reshape(count, rows, 128), near, 0, 0, axis_index_groups=plane)
    (mine,) = call(sum_kernel, [((far, rows, 128), BF16)], pieces)
    pieces = lax.all_to_all(mine, "z", 0, 0, axis_index_groups=line)
    (mine,) = call(sum_kernel, [((count, rows, 128), BF16)], pieces)
    return lax.all_to_all(mine, near, 0, 0, axis_index_groups=plane).reshape(ROWS, 128)


def local(volume, w_first, b_first, w_second, b_second, cotangent):
    cot = jnp.transpose(cotangent[0], (1, 2, 3, 0))
    w1 = jnp.transpose(w_first, (2, 3, 4, 1, 0)).reshape(27, C_IN, C_MID)
    w2 = jnp.transpose(w_second, (2, 3, 4, 1, 0)).reshape(27, C_MID, C_OUT)
    args = [pltpu.with_memory_space_constraint(a, pltpu.HBM) for a in (volume[0], cot, w1, b_first, w2, b_second)]
    across, inside, vol, cot, w1, b1, w2, b2 = call(
        pack_kernel,
        [((BLOCKS, 8, 128), BF16)] * 2 + [(a.shape, a.dtype) for a in args],
        *args,
        scratch=[pltpu.SemaphoreType.DMA((len(args),))],
        place=pltpu.HBM,
    )
    space = ("x", "core")
    count = lax.axis_size(space)
    pairs = [(i, i + 1) for i in range(1, count - 1, 2)]
    across = lax.ppermute(across, space, pairs + [(j, i) for i, j in pairs])
    inside = lax.all_gather(inside, "core")
    t1, t2, t2g = call(
        weights_kernel,
        [((256, 384), BF16), ((256, 1280), BF16), ((384, 768), BF16)],
        w1, b1, w2, b2,
    )
    feat, grads = call(
        main_kernel,
        [((2, 2, 32, C_OUT), BF16), ((ROWS, 128), BF16)],
        vol, across, inside, cot, t1, t2, t2g,
        scratch=[
            pltpu.VMEM((BLOCKS, 8, 128), BF16),
            pltpu.VMEM((BLOCKS, 8, 128), BF16),
            pltpu.VMEM((384, 2048), BF16),
            pltpu.VMEM((256, 1024), F32),
            pltpu.VMEM((1280, 512), BF16),
            pltpu.VMEM((768, 512), BF16),
            pltpu.VMEM((256, 1024), BF16),
        ],
    )
    grads = summed_over_devices(grads)
    gw1, gb1, gw2, gb2 = call(
        unpack_kernel,
        [((27, C_IN, C_MID), F32), ((1, C_MID), F32), ((27, C_MID, C_OUT), F32), ((1, C_OUT), F32)],
        grads,
    )
    gw1 = jnp.transpose(gw1.reshape(3, 3, 3, C_IN, C_MID), (4, 3, 0, 1, 2))
    gw2 = jnp.transpose(gw2.reshape(3, 3, 3, C_MID, C_OUT), (4, 3, 0, 1, 2))
    return jnp.transpose(feat, (3, 0, 1, 2))[None], gw1, gb1[0], gw2, gb2[0]


def solution(mesh):
    dp, space = mesh.devices.shape
    y = 4 if dp % 4 == 0 else 1
    grid = Mesh(mesh.devices.reshape(dp // y, y, space // 2, 2), ("z", "y", "x", "core"))
    data = P(("z", "y"), None, ("x", "core"), None, None)
    return jax.shard_map(
        local,
        mesh=grid,
        in_specs=(data, P(), P(), P(), P(), data),
        out_specs=(data, P(), P(), P(), P()),
        check_vma=False,
    )
```

```python
import jax
import jax.numpy as jnp
from jax import lax
from jax.experimental import pallas as pl
from jax.experimental.pallas import tpu as pltpu
from jax.sharding import Mesh, PartitionSpec as P

BF16, F32 = jnp.bfloat16, jnp.float32
VMEM = pl.BlockSpec(memory_space=pltpu.VMEM)
PARAMS = pltpu.CompilerParams(vmem_limit_bytes=48 * 1024 * 1024)
C_IN, C_MID, C_OUT, Y, X = 4, 32, 64, 8, 128
DEEP = 5
COT_AT = C_IN * DEEP
ONES_AT = COT_AT + 4
BLOCKS = ONES_AT + 1
ROWS_W2, ROWS_W1, ROWS_B2, ROWS_B1, ROWS = 0, 432, 480, 496, 512


def dot(a, b, dims=((1,), (0,))):
    return lax.dot_general(a, b, (dims, ((), ())), preferred_element_type=F32)


def iota(shape, dim):
    return lax.broadcasted_iota(jnp.int32, shape, dim)


def leaky(v):
    return jnp.maximum(v, 0.3 * v)


def rolled(v, shift):
    return pltpu.roll(v, shift, 1)


def paired(v):
    return ((v + rolled(v, v.shape[1] - 1)) * 0.125).astype(BF16)


def bias_scale():
    return 1.0 + iota((16, 128), 0).astype(F32) * 0.0625


def taps(v, period):
    place = iota(v.shape, 1) % period
    before = jnp.where(place == 0, 0.0, rolled(v, 1))
    after = jnp.where(place == period - 1, 0.0, rolled(v, v.shape[1] - 1))
    return before, v, after


def pack_kernel(vol_at, cot_at, w1_at, b1_at, w2_at, b2_at, across, inside, vol, cot, w1, b1, w2, b2, sems):
    pairs = ((vol_at, vol), (cot_at, cot), (w1_at, w1), (b1_at, b1), (w2_at, w2), (b2_at, b2))
    copies = [pltpu.make_async_copy(a, b, sems.at[i]) for i, (a, b) in enumerate(pairs)]
    for copy in copies:
        copy.start()
    across[ONES_AT] = jnp.ones((8, 128), BF16)
    inside[ONES_AT] = jnp.ones((8, 128), BF16)
    copies[0].wait()
    copies[1].wait()

    def fill(first, last):
        for c in range(C_IN):
            first[c * DEEP : (c + 1) * DEEP] = vol[c, :DEEP]
            last[c * DEEP : (c + 1) * DEEP] = vol[c, 8 - DEEP :]
        for ref, d in ((first, 0), (last, 1)):
            both = jnp.concatenate([cot[d, 0].astype(F32), cot[d, 1].astype(F32)], axis=1)
            ref[COT_AT:ONES_AT] = both.reshape(4, 8, 128).astype(BF16)

    core = lax.axis_index("core")
    pl.when(core == 0)(lambda: fill(across, inside))
    pl.when(core == 1)(lambda: fill(inside, across))
    for copy in copies[2:]:
        copy.wait()


def bias_rows(bias, copies):
    hi = bias.astype(BF16).astype(F32)
    lo = (bias - hi).astype(BF16).astype(F32)
    rest = bias - hi - lo
    hi, lo, rest = (jnp.concatenate([v] * copies, axis=1) for v in (hi, lo, rest))
    row = iota((128, 256), 0)
    zero = jnp.zeros((128, 256), F32)
    return jnp.where(row == 0, hi, jnp.where(row == 1, lo, jnp.where(row == 2, rest, zero)))


def weights_kernel(w1, b1, w2, b2, t1, t2, t2g):
    narrow = jnp.concatenate([w1[t].astype(F32) for t in range(27)], axis=0)
    wide = jnp.concatenate([narrow] * 4, axis=1)
    y_in = iota((8, 128), 0)
    lanes = iota((8, 128), 1) // C_MID
    blocks = []
    for kd in range(3):
        for kx in range(3):
            for c in range(C_IN):
                halves = []
                for half in range(2):
                    ky = y_in - (lanes + 4 * half) + 1
                    total = jnp.zeros((8, 128), F32)
                    for k in range(3):
                        at = ((kd * 3 + k) * 3 + kx) * C_IN + c
                        total = jnp.where(ky == k, wide[at : at + 1], total)
                    halves.append(total)
                blocks.append(jnp.concatenate(halves, axis=1))
    body = jnp.concatenate(blocks + [bias_rows(b1[...].reshape(1, C_MID), 8)[:96]], axis=0)
    t1[...] = body.astype(BF16).T
    nothing = jnp.zeros((C_MID, C_OUT), F32)
    for kd in range(3):
        for kx in range(3):
            w = [w2[(kd * 3 + ky) * 3 + kx].astype(F32) for ky in range(3)]
            pair = {
                a: jnp.concatenate([w[a] if a < 3 else nothing, w[a - 1] if a > 0 else nothing], axis=1)
                for a in range(4)
            }
            none = jnp.zeros((C_MID, 128), F32)
            block = jnp.concatenate(
                [
                    jnp.concatenate([pair.get(y - 2 * p + 1, none) for p in range(2)], axis=1)
                    for y in range(4)
                ],
                axis=0,
            )
            t2g[kd * 128 : (kd + 1) * 128, kx * 256 : (kx + 1) * 256] = block.astype(BF16)
            at = (kd * 3 + kx) * 128
            t2[:, at : at + 128] = block.astype(BF16).T
    t2[:, 1152:] = bias_rows(b2[...].reshape(1, C_OUT), 4).T.astype(BF16)


def main_kernel(vol, across, inside, cot, t1, t2, t2g, feat, grads, before, behind, p1, pre1, p2, g4x, g1):
    def place(first, second):
        before[...] = first[...]
        behind[...] = second[...]

    core = lax.axis_index("core")
    pl.when(core == 0)(lambda: place(across, inside.at[1]))
    pl.when(core == 1)(lambda: place(inside.at[0], across))
    lane = iota((1, 128), 1)
    low = lane < 64

    for z in range(-5, 13):
        def plane(c):
            if z < 0:
                return before[c * DEEP + z + 5]
            if z >= 8:
                return behind[c * DEEP + z - 8]
            return vol[c, z]
        v = jnp.concatenate([plane(c).astype(F32) for c in range(C_IN)], axis=0)
        stack = jnp.concatenate(taps(v, 128), axis=0).astype(BF16)
        for kd in range(3):
            to = z - kd + 1 + 4
            if 0 <= to < 16:
                p1[kd * 96 : (kd + 1) * 96, to * 128 : (to + 1) * 128] = stack
    p1[288:, :] = jnp.ones((96, 2048), BF16)

    pooled = []
    for d in range(8):
        pre = dot(t1[...], p1[:, d * 256 : (d + 1) * 256])
        if 2 <= d < 6:
            pre1[:, (d - 2) * 256 : (d - 1) * 256] = pre
        act = leaky(pre).reshape(4, 2, C_MID, 256)
        act = (act[:, 0] + act[:, 1]).reshape(128, 256)
        pooled.append(paired(act[:, :128] + act[:, 128:]))

    row, col = iota((256, 128), 0), iota((256, 128), 1)
    pool = jnp.where((row // 128 == col // 64) & (row % 128 == col % 64 * 2), 1.0, 0.0).astype(BF16)
    m_before = before[ONES_AT].astype(F32)[:1]
    m_behind = behind[ONES_AT].astype(F32)[:1]
    pairs = [jnp.concatenate([pooled[r], pooled[r + 2]], axis=1) for r in range(6)]
    chosen = dot(jnp.concatenate(pairs, axis=0), pool)
    for r in range(6):
        act = chosen[r * 128 : (r + 1) * 128]
        if r < 2:
            act = act * jnp.where(low, m_before, 1.0)
        if r >= 4:
            act = act * jnp.where(low, 1.0, m_behind)
        stack = jnp.concatenate(taps(act, 64), axis=0).astype(BF16)
        for kd in range(3):
            to = r - kd
            if 0 <= to < 4:
                p2[kd * 384 : (kd + 1) * 384, to * 128 : (to + 1) * 128] = stack
    p2[1152:, :] = jnp.ones((128, 512), BF16)

    pre2 = dot(t2[...], p2[...])

    pieces = [before[COT_AT:ONES_AT].astype(F32).reshape(32, 128)]
    for d in range(2):
        pieces.append(jnp.concatenate([cot[d, 0].astype(F32), cot[d, 1].astype(F32)], axis=1))
    pieces.append(behind[COT_AT:ONES_AT].astype(F32).reshape(32, 128))
    cots = jnp.concatenate(pieces, axis=0).T.astype(BF16)
    row, col = iota((128, 384), 0), iota((128, 384), 1)
    spread = jnp.where((row // 32 == col // 128 + col % 128 // 64) & (row % 32 == col % 64 // 2), 0.125, 0.0)
    up = dot(cots, spread.astype(BF16))
    up = jnp.concatenate([up[:, :256], up[:, 128:]], axis=1).reshape(2, 1, C_OUT, 512)
    mask = pre2.reshape(2, 2, C_OUT, 512) > 0.0
    grad = jnp.where(mask, up, 0.3 * up).reshape(256, 512).astype(BF16)
    for r in range(4):
        piece = grad[:, r * 128 : (r + 1) * 128].astype(F32)
        for kx, tap in enumerate(reversed(taps(piece, 64))):
            g4x[kx * 256 : (kx + 1) * 256, r * 128 : (r + 1) * 128] = tap.astype(BF16)

    act = leaky(pre2[:, 128:384]).reshape(2, 2, C_OUT, 256)
    act = act[:, 0] + act[:, 1]
    act = act[:, :, :128] + act[:, :, 128:]
    row, col = iota((64, 128), 0), iota((64, 128), 1)
    pool = jnp.where((row // 32 == col // 64) & (row % 32 * 2 == col % 64), 1.0, 0.0).astype(BF16)
    for y in range(2):
        out = dot(pool, paired(act[y]), ((1,), (1,)))
        for d in range(2):
            feat[d, y] = out[d * 32 : (d + 1) * 32].astype(BF16)

    early = dot(t2g[128:384], g4x[:, 0:256])
    late = dot(t2g[0:256], g4x[:, 256:512])
    back = jnp.concatenate([early[:128, 128:] + early[128:, :128], early[128:, 128:] + late[128:, :128]], axis=1)
    back = back + late[:128]
    one = back * 0.125
    less = 0.3 * one
    stack = jnp.concatenate([one[:, :128], one[:, 128:], less[:, :128], less[:, 128:]], axis=0)
    row, col = iota((128, 256), 0), iota((128, 256), 1)
    spread = jnp.where(row == col // 128 * 64 + col % 128 // 2, 1.0, 0.0).astype(BF16)
    wide = dot(stack.astype(BF16), spread)
    for z in range(8):
        a = z // 2
        at, half = (a % 2) * 128, (a // 2) * 128
        yes = wide[at : at + 128, half : half + 128].reshape(4, 1, C_MID, 128)
        no = wide[256 + at : 384 + at, half : half + 128].reshape(4, 1, C_MID, 128)
        mask = pre1[:, z * 128 : (z + 1) * 128].reshape(4, 2, C_MID, 128) > 0.0
        g1[:, z * 128 : (z + 1) * 128] = jnp.where(mask, yes, no).reshape(256, 128).astype(BF16)

    d2 = dot(p2[0:1168, 128:384], g4x[256:512, 128:384], ((1,), (1,)))
    for kd in range(3):
        for kx in range(3):
            base = (kd * 3 + kx) * 128
            def block(y, p):
                return d2[base + y * 32 : base + (y + 1) * 32, p * 128 : (p + 1) * 128]
            for ky in range(3):
                even = [block(y, p) for p in range(2) for y in [2 * p + ky - 1] if 0 <= y < 4]
                odd = [block(y, p) for p in range(2) for y in [2 * p + ky] if 0 <= y < 4]
                total = sum(even[1:], even[0]) + rolled(sum(odd[1:], odd[0]), 64)
                at = ROWS_W2 + ((kd * 3 + ky) * 3 + kx) * 16
                grads[at : at + 16] = jnp.where(low, total[:16], rolled(total[16:], 64)).astype(BF16)
    scale = bias_scale()
    bias = d2[1152:1168, :128] + d2[1152:1168, 128:]
    grads[ROWS_B2 : ROWS_B2 + 16] = ((bias + rolled(bias, 64)) * scale).astype(BF16)

    d1 = dot(p1[0:304, 512:1536], g1[...], ((1,), (1,)))
    body = d1[:288].reshape(36, 8, 256)
    ky = iota((1, 8, 256), 1) - iota((1, 8, 256), 2) // C_MID + 1
    total = jnp.zeros((36, 128), F32)
    for k in range(3):
        part = jnp.sum(jnp.where(ky == k, body, 0.0), axis=1)
        part = part[:, :128] + part[:, 128:]
        part = part + rolled(part, 64)
        part = part + rolled(part, 32)
        total = jnp.where(lane // 32 == k, part, total)
    total = jnp.concatenate([total, jnp.zeros((12, 128), F32)], axis=0)
    grads[ROWS_W1 : ROWS_W1 + 48] = total.astype(BF16)
    bias = d1[288:304, :128] + d1[288:304, 128:]
    bias = bias + rolled(bias, 64)
    grads[ROWS_B1 : ROWS_B1 + 16] = ((bias + rolled(bias, 32)) * scale).astype(BF16)


def unpack_kernel(grads, w1, b1, w2, b2):
    for t in range(27):
        block = grads[t * 16 : (t + 1) * 16].astype(F32)
        w2[t, 0:16] = block[:, :64]
        w2[t, 16:32] = rolled(block, 64)[:, :64]
    body = grads[ROWS_W1 : ROWS_W1 + 48].astype(F32)
    for ky in range(3):
        part = rolled(body, (128 - 32 * ky) % 128) if ky else body
        for kd in range(3):
            for kx in range(3):
                at = (kd * 3 + kx) * C_IN
                w1[(kd * 3 + ky) * 3 + kx] = part[at : at + C_IN, :C_MID]
    weigh = 1.0 / (16.0 * bias_scale())
    body = grads[ROWS_B2 : ROWS_B2 + 16].astype(F32) * weigh
    b2[...] = jnp.sum(body, axis=0, keepdims=True)[:, :C_OUT]
    body = grads[ROWS_B1 : ROWS_B1 + 16].astype(F32) * weigh
    b1[...] = jnp.sum(body, axis=0, keepdims=True)[:, :C_MID]


def call(kernel, outs, *args, scratch=(), place=pltpu.VMEM):
    return pl.pallas_call(
        kernel,
        out_shape=[jax.ShapeDtypeStruct(s, t) for s, t in outs],
        in_specs=[pl.BlockSpec(memory_space=place)] * len(args),
        out_specs=[VMEM] * len(outs),
        scratch_shapes=scratch,
        compiler_params=PARAMS,
    )(*args)


def sum_kernel(pieces, out):
    total = pieces[0].astype(F32)
    for i in range(1, pieces.shape[0]):
        total = total + pieces[i].astype(F32)
    total = total.astype(BF16)
    for i in range(out.shape[0]):
        out[i] = total


def rounded(count, first):
    return [[(first + i) % count for i in range(count)]]


def farthest(count, first):
    return [sorted(range(count), key=lambda i: (i != first, -min((i - first) % count, (first - i) % count)))]


def summed_over_devices(grads):
    near = ("y", "x", "core")
    y, x, core = (lax.axis_size(axis) for axis in near)
    count, far = y * x * core, lax.axis_size("z")
    plane = rounded(count, (y // 2 * x + x // 2) * core + 1)
    line = farthest(far, far // 2 + 1)
    rows = ROWS // count
    pieces = lax.all_to_all(grads.reshape(count, rows, 128), near, 0, 0, axis_index_groups=plane)
    (mine,) = call(sum_kernel, [((far, rows, 128), BF16)], pieces)
    pieces = lax.all_to_all(mine, "z", 0, 0, axis_index_groups=line)
    (mine,) = call(sum_kernel, [((count, rows, 128), BF16)], pieces)
    return lax.all_to_all(mine, near, 0, 0, axis_index_groups=plane).reshape(ROWS, 128)


def local(volume, w_first, b_first, w_second, b_second, cotangent):
    cot = jnp.transpose(cotangent[0], (1, 2, 3, 0))
    w1 = jnp.transpose(w_first, (2, 3, 4, 1, 0)).reshape(27, C_IN, C_MID)
    w2 = jnp.transpose(w_second, (2, 3, 4, 1, 0)).reshape(27, C_MID, C_OUT)
    args = [pltpu.with_memory_space_constraint(a, pltpu.HBM) for a in (volume[0], cot, w1, b_first, w2, b_second)]
    across, inside, vol, cot, w1, b1, w2, b2 = call(
        pack_kernel,
        [((BLOCKS, 8, 128), BF16)] * 2 + [(a.shape, a.dtype) for a in args],
        *args,
        scratch=[pltpu.SemaphoreType.DMA((len(args),))],
        place=pltpu.HBM,
    )
    space = ("x", "core")
    count = lax.axis_size(space)
    pairs = [(i, i + 1) for i in range(1, count - 1, 2)]
    across = lax.ppermute(across, space, pairs + [(j, i) for i, j in pairs])
    inside = lax.all_gather(inside, "core")
    t1, t2, t2g = call(
        weights_kernel,
        [((256, 384), BF16), ((256, 1280), BF16), ((384, 768), BF16)],
        w1, b1, w2, b2,
    )
    feat, grads = call(
        main_kernel,
        [((2, 2, 32, C_OUT), BF16), ((ROWS, 128), BF16)],
        vol, across, inside, cot, t1, t2, t2g,
        scratch=[
            pltpu.VMEM((BLOCKS, 8, 128), BF16),
            pltpu.VMEM((BLOCKS, 8, 128), BF16),
            pltpu.VMEM((384, 2048), BF16),
            pltpu.VMEM((256, 1024), F32),
            pltpu.VMEM((1280, 512), BF16),
            pltpu.VMEM((768, 512), BF16),
            pltpu.VMEM((256, 1024), BF16),
        ],
    )
    grads = summed_over_devices(grads)
    gw1, gb1, gw2, gb2 = call(
        unpack_kernel,
        [((27, C_IN, C_MID), F32), ((1, C_MID), F32), ((27, C_MID, C_OUT), F32), ((1, C_OUT), F32)],
        grads,
    )
    gw1 = jnp.transpose(gw1.reshape(3, 3, 3, C_IN, C_MID), (4, 3, 0, 1, 2))
    gw2 = jnp.transpose(gw2.reshape(3, 3, 3, C_MID, C_OUT), (4, 3, 0, 1, 2))
    return jnp.transpose(feat, (3, 0, 1, 2))[None], gw1, gb1[0], gw2, gb2[0]


def solution(mesh):
    dp, space = mesh.devices.shape
    y = 4 if dp % 4 == 0 else 1
    grid = Mesh(mesh.devices.reshape(dp // y, y, space // 2, 2), ("z", "y", "x", "core"))
    data = P(("z", "y"), None, ("x", "core"), None, None)
    return jax.shard_map(
        local,
        mesh=grid,
        in_specs=(data, P(), P(), P(), P(), data),
        out_specs=(data, P(), P(), P(), P()),
        check_vma=False,
    )
```

```python
import jax
import jax.numpy as jnp
from jax import lax
from jax.experimental import pallas as pl
from jax.experimental.pallas import tpu as pltpu
from jax.sharding import Mesh, PartitionSpec as P

BF16, F32 = jnp.bfloat16, jnp.float32
VMEM = pl.BlockSpec(memory_space=pltpu.VMEM)
PARAMS = pltpu.CompilerParams(vmem_limit_bytes=48 * 1024 * 1024)
C_IN, C_MID, C_OUT, Y, X = 4, 32, 64, 8, 128
DEEP = 5
COT_AT = C_IN * DEEP
ONES_AT = COT_AT + 4
BLOCKS = ONES_AT + 1
ROWS_W2, ROWS_W1, ROWS_B2, ROWS_B1, ROWS = 0, 432, 480, 496, 512


def dot(a, b, dims=((1,), (0,))):
    return lax.dot_general(a, b, (dims, ((), ())), preferred_element_type=F32)


def iota(shape, dim):
    return lax.broadcasted_iota(jnp.int32, shape, dim)


def leaky(v):
    return jnp.maximum(v, 0.3 * v)


def rolled(v, shift):
    return pltpu.roll(v, shift, 1)


def paired(v):
    return ((v + rolled(v, v.shape[1] - 1)) * 0.125).astype(BF16)


def bias_scale():
    return 1.0 + iota((16, 128), 0).astype(F32) * 0.0625


def taps(v, period):
    place = iota(v.shape, 1) % period
    before = jnp.where(place == 0, 0.0, rolled(v, 1))
    after = jnp.where(place == period - 1, 0.0, rolled(v, v.shape[1] - 1))
    return before, v, after


def pack_kernel(vol_at, cot_at, w1_at, b1_at, w2_at, b2_at, across, inside, vol, cot, w1, b1, w2, b2, sems):
    pairs = ((vol_at, vol), (cot_at, cot), (w1_at, w1), (b1_at, b1), (w2_at, w2), (b2_at, b2))
    copies = [pltpu.make_async_copy(a, b, sems.at[i]) for i, (a, b) in enumerate(pairs)]
    for copy in copies:
        copy.start()
    across[ONES_AT] = jnp.ones((8, 128), BF16)
    inside[ONES_AT] = jnp.ones((8, 128), BF16)
    copies[0].wait()
    copies[1].wait()

    def fill(first, last):
        for c in range(C_IN):
            first[c * DEEP : (c + 1) * DEEP] = vol[c, :DEEP]
            last[c * DEEP : (c + 1) * DEEP] = vol[c, 8 - DEEP :]
        for ref, d in ((first, 0), (last, 1)):
            both = jnp.concatenate([cot[d, 0].astype(F32), cot[d, 1].astype(F32)], axis=1)
            ref[COT_AT:ONES_AT] = both.reshape(4, 8, 128).astype(BF16)

    core = lax.axis_index("core")
    pl.when(core == 0)(lambda: fill(across, inside))
    pl.when(core == 1)(lambda: fill(inside, across))
    for copy in copies[2:]:
        copy.wait()


def bias_rows(bias, copies):
    hi = bias.astype(BF16).astype(F32)
    lo = (bias - hi).astype(BF16).astype(F32)
    rest = bias - hi - lo
    hi, lo, rest = (jnp.concatenate([v] * copies, axis=1) for v in (hi, lo, rest))
    row = iota((128, 256), 0)
    zero = jnp.zeros((128, 256), F32)
    return jnp.where(row == 0, hi, jnp.where(row == 1, lo, jnp.where(row == 2, rest, zero)))


def weights_kernel(w1, b1, w2, b2, t1, t2, t2g):
    narrow = jnp.concatenate([w1[t].astype(F32) for t in range(27)], axis=0)
    wide = jnp.concatenate([narrow] * 4, axis=1)
    y_in = iota((8, 128), 0)
    lanes = iota((8, 128), 1) // C_MID
    blocks = []
    for kd in range(3):
        for kx in range(3):
            for c in range(C_IN):
                halves = []
                for half in range(2):
                    ky = y_in - (lanes + 4 * half) + 1
                    total = jnp.zeros((8, 128), F32)
                    for k in range(3):
                        at = ((kd * 3 + k) * 3 + kx) * C_IN + c
                        total = jnp.where(ky == k, wide[at : at + 1], total)
                    halves.append(total)
                blocks.append(jnp.concatenate(halves, axis=1))
    body = jnp.concatenate(blocks + [bias_rows(b1[...].reshape(1, C_MID), 8)[:96]], axis=0)
    t1[...] = body.astype(BF16).T
    nothing = jnp.zeros((C_MID, C_OUT), BF16)
    for kd in range(3):
        for kx in range(3):
            w = [w2[(kd * 3 + ky) * 3 + kx] for ky in range(3)]
            pair = {
                a: jnp.concatenate([w[a] if a < 3 else nothing, w[a - 1] if a > 0 else nothing], axis=1)
                for a in range(4)
            }
            none = jnp.zeros((C_MID, 128), BF16)
            block = jnp.concatenate(
                [
                    jnp.concatenate([pair.get(y - 2 * p + 1, none) for p in range(2)], axis=1)
                    for y in range(4)
                ],
                axis=0,
            )
            t2g[kd * 128 : (kd + 1) * 128, kx * 256 : (kx + 1) * 256] = block
            at = (kd * 3 + kx) * 128
            t2[:, at : at + 128] = block.T
    t2[:, 1152:] = bias_rows(b2[...].reshape(1, C_OUT), 4).T.astype(BF16)


def main_kernel(vol, across, inside, cot, t1, t2, t2g, feat, grads, before, behind, p1, pre1, p2, g4x, g1):
    def place(first, second):
        before[...] = first[...]
        behind[...] = second[...]

    core = lax.axis_index("core")
    pl.when(core == 0)(lambda: place(across, inside.at[1]))
    pl.when(core == 1)(lambda: place(inside.at[0], across))
    lane = iota((1, 128), 1)
    low = lane < 64

    for z in range(-5, 13):
        def plane(c):
            if z < 0:
                return before[c * DEEP + z + 5]
            if z >= 8:
                return behind[c * DEEP + z - 8]
            return vol[c, z]
        v = jnp.concatenate([plane(c).astype(F32) for c in range(C_IN)], axis=0)
        stack = jnp.concatenate(taps(v, 128), axis=0).astype(BF16)
        for kd in range(3):
            to = z - kd + 1 + 4
            if 0 <= to < 16:
                p1[kd * 96 : (kd + 1) * 96, to * 128 : (to + 1) * 128] = stack
    p1[288:, :] = jnp.ones((96, 2048), BF16)

    pooled = []
    for d in range(8):
        pre = dot(t1[...], p1[:, d * 256 : (d + 1) * 256])
        if 2 <= d < 6:
            pre1[:, (d - 2) * 256 : (d - 1) * 256] = pre
        act = leaky(pre).reshape(4, 2, C_MID, 256)
        act = (act[:, 0] + act[:, 1]).reshape(128, 256)
        pooled.append(paired(act[:, :128] + act[:, 128:]))

    row, col = iota((256, 128), 0), iota((256, 128), 1)
    pool = jnp.where((row // 128 == col // 64) & (row % 128 == col % 64 * 2), 1.0, 0.0).astype(BF16)
    m_before = before[ONES_AT].astype(F32)[:1]
    m_behind = behind[ONES_AT].astype(F32)[:1]
    pairs = [jnp.concatenate([pooled[r], pooled[r + 2]], axis=1) for r in range(6)]
    chosen = dot(jnp.concatenate(pairs, axis=0), pool)
    for r in range(6):
        act = chosen[r * 128 : (r + 1) * 128]
        if r < 2:
            act = act * jnp.where(low, m_before, 1.0)
        if r >= 4:
            act = act * jnp.where(low, 1.0, m_behind)
        stack = jnp.concatenate(taps(act, 64), axis=0).astype(BF16)
        for kd in range(3):
            to = r - kd
            if 0 <= to < 4:
                p2[kd * 384 : (kd + 1) * 384, to * 128 : (to + 1) * 128] = stack
    p2[1152:, :] = jnp.ones((128, 512), BF16)

    pre2 = dot(t2[...], p2[...])

    pieces = [before[COT_AT:ONES_AT].astype(F32).reshape(32, 128)]
    for d in range(2):
        pieces.append(jnp.concatenate([cot[d, 0].astype(F32), cot[d, 1].astype(F32)], axis=1))
    pieces.append(behind[COT_AT:ONES_AT].astype(F32).reshape(32, 128))
    cots = jnp.concatenate(pieces, axis=0).T.astype(BF16)
    row, col = iota((128, 384), 0), iota((128, 384), 1)
    spread = jnp.where((row // 32 == col // 128 + col % 128 // 64) & (row % 32 == col % 64 // 2), 0.125, 0.0)
    up = dot(cots, spread.astype(BF16))
    up = jnp.concatenate([up[:, :256], up[:, 128:]], axis=1).reshape(2, 1, C_OUT, 512)
    mask = pre2.reshape(2, 2, C_OUT, 512) > 0.0
    grad = jnp.where(mask, up, 0.3 * up).reshape(256, 512).astype(BF16)
    for r in range(4):
        piece = grad[:, r * 128 : (r + 1) * 128].astype(F32)
        for kx, tap in enumerate(reversed(taps(piece, 64))):
            g4x[kx * 256 : (kx + 1) * 256, r * 128 : (r + 1) * 128] = tap.astype(BF16)

    act = leaky(pre2[:, 128:384]).reshape(2, 2, C_OUT, 256)
    act = act[:, 0] + act[:, 1]
    act = act[:, :, :128] + act[:, :, 128:]
    row, col = iota((64, 128), 0), iota((64, 128), 1)
    pool = jnp.where((row // 32 == col // 64) & (row % 32 * 2 == col % 64), 1.0, 0.0).astype(BF16)
    for y in range(2):
        out = dot(pool, paired(act[y]), ((1,), (1,)))
        for d in range(2):
            feat[d, y] = out[d * 32 : (d + 1) * 32].astype(BF16)

    early = dot(t2g[128:384], g4x[:, 0:256])
    late = dot(t2g[0:256], g4x[:, 256:512])
    back = jnp.concatenate([early[:128, 128:] + early[128:, :128], early[128:, 128:] + late[128:, :128]], axis=1)
    back = back + late[:128]
    one = back * 0.125
    less = 0.3 * one
    stack = jnp.concatenate([one[:, :128], one[:, 128:], less[:, :128], less[:, 128:]], axis=0)
    row, col = iota((128, 256), 0), iota((128, 256), 1)
    spread = jnp.where(row == col // 128 * 64 + col % 128 // 2, 1.0, 0.0).astype(BF16)
    wide = dot(stack.astype(BF16), spread)
    for z in range(8):
        a = z // 2
        at, half = (a % 2) * 128, (a // 2) * 128
        yes = wide[at : at + 128, half : half + 128].reshape(4, 1, C_MID, 128)
        no = wide[256 + at : 384 + at, half : half + 128].reshape(4, 1, C_MID, 128)
        mask = pre1[:, z * 128 : (z + 1) * 128].reshape(4, 2, C_MID, 128) > 0.0
        g1[:, z * 128 : (z + 1) * 128] = jnp.where(mask, yes, no).reshape(256, 128).astype(BF16)

    d2 = dot(p2[0:1168, 128:384], g4x[256:512, 128:384], ((1,), (1,)))
    for kd in range(3):
        for kx in range(3):
            base = (kd * 3 + kx) * 128
            def block(y, p):
                return d2[base + y * 32 : base + (y + 1) * 32, p * 128 : (p + 1) * 128]
            for ky in range(3):
                even = [block(y, p) for p in range(2) for y in [2 * p + ky - 1] if 0 <= y < 4]
                odd = [block(y, p) for p in range(2) for y in [2 * p + ky] if 0 <= y < 4]
                total = sum(even[1:], even[0]) + rolled(sum(odd[1:], odd[0]), 64)
                at = ROWS_W2 + ((kd * 3 + ky) * 3 + kx) * 16
                grads[at : at + 16] = jnp.where(low, total[:16], rolled(total[16:], 64)).astype(BF16)
    scale = bias_scale()
    bias = d2[1152:1168, :128] + d2[1152:1168, 128:]
    grads[ROWS_B2 : ROWS_B2 + 16] = ((bias + rolled(bias, 64)) * scale).astype(BF16)

    d1 = dot(p1[0:304, 512:1536], g1[...], ((1,), (1,)))
    body = d1[:288].reshape(36, 8, 256)
    ky = iota((1, 8, 256), 1) - iota((1, 8, 256), 2) // C_MID + 1
    total = jnp.zeros((36, 128), F32)
    for k in range(3):
        part = jnp.sum(jnp.where(ky == k, body, 0.0), axis=1)
        part = part[:, :128] + part[:, 128:]
        part = part + rolled(part, 64)
        part = part + rolled(part, 32)
        total = jnp.where(lane // 32 == k, part, total)
    total = jnp.concatenate([total, jnp.zeros((12, 128), F32)], axis=0)
    grads[ROWS_W1 : ROWS_W1 + 48] = total.astype(BF16)
    bias = d1[288:304, :128] + d1[288:304, 128:]
    bias = bias + rolled(bias, 64)
    grads[ROWS_B1 : ROWS_B1 + 16] = ((bias + rolled(bias, 32)) * scale).astype(BF16)


def unpack_kernel(grads, w1, b1, w2, b2):
    for t in range(27):
        block = grads[t * 16 : (t + 1) * 16].astype(F32)
        w2[t, 0:16] = block[:, :64]
        w2[t, 16:32] = rolled(block, 64)[:, :64]
    body = grads[ROWS_W1 : ROWS_W1 + 48].astype(F32)
    for ky in range(3):
        part = rolled(body, (128 - 32 * ky) % 128) if ky else body
        for kd in range(3):
            for kx in range(3):
                at = (kd * 3 + kx) * C_IN
                w1[(kd * 3 + ky) * 3 + kx] = part[at : at + C_IN, :C_MID]
    weigh = 1.0 / (16.0 * bias_scale())
    body = grads[ROWS_B2 : ROWS_B2 + 16].astype(F32) * weigh
    b2[...] = jnp.sum(body, axis=0, keepdims=True)[:, :C_OUT]
    body = grads[ROWS_B1 : ROWS_B1 + 16].astype(F32) * weigh
    b1[...] = jnp.sum(body, axis=0, keepdims=True)[:, :C_MID]


def call(kernel, outs, *args, scratch=(), place=pltpu.VMEM):
    return pl.pallas_call(
        kernel,
        out_shape=[jax.ShapeDtypeStruct(s, t) for s, t in outs],
        in_specs=[pl.BlockSpec(memory_space=place)] * len(args),
        out_specs=[VMEM] * len(outs),
        scratch_shapes=scratch,
        compiler_params=PARAMS,
    )(*args)


def sum_kernel(pieces, out):
    total = pieces[0].astype(F32)
    for i in range(1, pieces.shape[0]):
        total = total + pieces[i].astype(F32)
    total = total.astype(BF16)
    for i in range(out.shape[0]):
        out[i] = total


def rounded(count, first):
    return [[(first + i) % count for i in range(count)]]


def farthest(count, first):
    return [sorted(range(count), key=lambda i: (i != first, -min((i - first) % count, (first - i) % count)))]


def summed_over_devices(grads):
    near = ("y", "x", "core")
    y, x, core = (lax.axis_size(axis) for axis in near)
    count, far = y * x * core, lax.axis_size("z")
    plane = rounded(count, (y // 2 * x + x // 2) * core + 1)
    line = farthest(far, far // 2 + 1)
    rows = ROWS // count
    pieces = lax.all_to_all(grads.reshape(count, rows, 128), near, 0, 0, axis_index_groups=plane)
    (mine,) = call(sum_kernel, [((far, rows, 128), BF16)], pieces)
    pieces = lax.all_to_all(mine, "z", 0, 0, axis_index_groups=line)
    (mine,) = call(sum_kernel, [((count, rows, 128), BF16)], pieces)
    return lax.all_to_all(mine, near, 0, 0, axis_index_groups=plane).reshape(ROWS, 128)


def local(volume, w_first, b_first, w_second, b_second, cotangent):
    cot = jnp.transpose(cotangent[0], (1, 2, 3, 0))
    w1 = jnp.transpose(w_first, (2, 3, 4, 1, 0)).reshape(27, C_IN, C_MID)
    w2 = jnp.transpose(w_second, (2, 3, 4, 1, 0)).reshape(27, C_MID, C_OUT)
    args = [pltpu.with_memory_space_constraint(a, pltpu.HBM) for a in (volume[0], cot, w1, b_first, w2, b_second)]
    across, inside, vol, cot, w1, b1, w2, b2 = call(
        pack_kernel,
        [((BLOCKS, 8, 128), BF16)] * 2 + [(a.shape, a.dtype) for a in args],
        *args,
        scratch=[pltpu.SemaphoreType.DMA((len(args),))],
        place=pltpu.HBM,
    )
    space = ("x", "core")
    count = lax.axis_size(space)
    pairs = [(i, i + 1) for i in range(1, count - 1, 2)]
    across = lax.ppermute(across, space, pairs + [(j, i) for i, j in pairs])
    inside = lax.all_gather(inside, "core")
    t1, t2, t2g = call(
        weights_kernel,
        [((256, 384), BF16), ((256, 1280), BF16), ((384, 768), BF16)],
        w1, b1, w2, b2,
    )
    feat, grads = call(
        main_kernel,
        [((2, 2, 32, C_OUT), BF16), ((ROWS, 128), BF16)],
        vol, across, inside, cot, t1, t2, t2g,
        scratch=[
            pltpu.VMEM((BLOCKS, 8, 128), BF16),
            pltpu.VMEM((BLOCKS, 8, 128), BF16),
            pltpu.VMEM((384, 2048), BF16),
            pltpu.VMEM((256, 1024), F32),
            pltpu.VMEM((1280, 512), BF16),
            pltpu.VMEM((768, 512), BF16),
            pltpu.VMEM((256, 1024), BF16),
        ],
    )
    grads = summed_over_devices(grads)
    gw1, gb1, gw2, gb2 = call(
        unpack_kernel,
        [((27, C_IN, C_MID), F32), ((1, C_MID), F32), ((27, C_MID, C_OUT), F32), ((1, C_OUT), F32)],
        grads,
    )
    gw1 = jnp.transpose(gw1.reshape(3, 3, 3, C_IN, C_MID), (4, 3, 0, 1, 2))
    gw2 = jnp.transpose(gw2.reshape(3, 3, 3, C_MID, C_OUT), (4, 3, 0, 1, 2))
    return jnp.transpose(feat, (3, 0, 1, 2))[None], gw1, gb1[0], gw2, gb2[0]


def solution(mesh):
    dp, space = mesh.devices.shape
    y = 4 if dp % 4 == 0 else 1
    grid = Mesh(mesh.devices.reshape(dp // y, y, space // 2, 2), ("z", "y", "x", "core"))
    data = P(("z", "y"), None, ("x", "core"), None, None)
    return jax.shard_map(
        local,
        mesh=grid,
        in_specs=(data, P(), P(), P(), P(), data),
        out_specs=(data, P(), P(), P(), P()),
        check_vma=False,
    )
```
